128 devices in a mesh: node: 16 (over z, x), local: 8 (over y, core).
Axes of the slice: x: 4, y: 4, z: 4, core: 2. Of those that a mesh axis runs over, the one named last changes fastest.
Arguments:
- tokens: bfloat16 [16384, 3584], P(('node', 'local')), may hold values from -6 to 6
- grad_out: bfloat16 [16384, 3584], P(('node', 'local')), may hold values from -6 to 6
- expert_ids: int32 [16384, 1], P(('node', 'local')), may hold values from 0 to 31; in each aligned block of 128 rows (0 to 127, 128 to 255, ...) at most 5 rows name the same one
- route_gate: bfloat16 [16384, 1], P(('node', 'local')), may hold values from 0.25 to 2.5
- expert_gate: bfloat16 [128, 3584, 256], P(('node', 'local')), may hold values from -0.09375 to 0.09375
- expert_up: bfloat16 [128, 3584, 256], P(('node', 'local')), may hold values from -0.09375 to 0.09375
- expert_down: bfloat16 [128, 256, 3584], P(('node', 'local')), may hold values from -0.1875 to 0.1875
- shared_gate: bfloat16 [3584, 1024], P(None, 'local'), may hold values from -0.09375 to 0.09375
- shared_up: bfloat16 [3584, 1024], P(None, 'local'), may hold values from -0.09375 to 0.09375
- shared_down: bfloat16 [1024, 3584], P('local'), may hold values from -0.1875 to 0.1875
Outputs:
- grad_tokens: bfloat16 [16384, 3584], P(('node', 'local'))
- d_expert_gate: bfloat16 [128, 3584, 256], P(('node', 'local'))
- d_expert_up: bfloat16 [128, 3584, 256], P(('node', 'local'))
- d_expert_down: bfloat16 [128, 256, 3584], P(('node', 'local'))
- d_shared_gate: bfloat16 [3584, 1024], P(None, 'local')
- d_shared_up: bfloat16 [3584, 1024], P(None, 'local')
- d_shared_down: bfloat16 [1024, 3584], P('local')
The draws below stay inside these ranges and needn't reach their ends.
Inputs may be any that keep to these rules, and one draw needn't show every extreme that they name: `expert_ids`: the 128 tokens of one device choose any one expert at most 5 times, and on some devices some expert exactly 5 times.
All inputs are finite; a program needn't handle non-finite values.
Results may differ from the reference program's by a relative error of at most 0.019.
Values may be sent and summed in bfloat16 or wider, within the bound.
No kernel may reach another device: no remote copies, remote signals or barrier semaphores. Data moves between devices by JAX's collectives and lax.ppermute only.
A program may use at most 192 MiB of HBM per device.

```python
import math
import jax
import jax.numpy as jnp
import numpy as np
from jax import lax

D = 3584
HID = 1024
SH = 1024
TOPK = 1
TOK_DEV = 128
EXPERTS = 32
CAPD = 5
TOKENS = 16384
N_LOCAL = 8
DEVICES = 128


def steps_of(own_key, shape, cuts, low, high):
    level, own = 1.0, jax.random.fold_in(own_key, 6)
    for axis_at, shards_of in cuts:
        draws = jnp.exp(jax.random.uniform(jax.random.fold_in(own, axis_at), (shards_of,), jnp.float32, low / len(cuts), high / len(cuts)))
        level = level * jnp.repeat(draws, shape[axis_at] // shards_of).reshape([-1 if axis == axis_at else 1 for axis in range(len(shape))])
    return level


def deal_out(key, own, number, rows, amount, top, most, lean):
    sequence = jax.random.permutation(key, amount)
    crowded, usual = load_shares(amount, rows * top, most, lean, True), load_shares(amount, rows * top, most, lean, False)
    places = jnp.arange(amount)

    def named(lengths, rotation):
        used = int((lengths > 0).sum())
        fixed = max(1, used // 4)
        shifted = fixed + (places - fixed + rotation * (used - fixed)) % max(1, amount - fixed)
        return jnp.zeros((amount,), jnp.int32).at[sequence[jnp.where(places < fixed, places, shifted)]].set(jnp.asarray(lengths, jnp.int32))

    lengths = jnp.where(number % 4 == 0, named(crowded, number // 4), named(usual, number - number // 4 - 1))
    mixed = jax.random.permutation(jax.random.fold_in(own, 3), amount)
    donor, sink = mixed[0:amount // 2 * 2:2], mixed[1:amount // 2 * 2:2]
    slack = jnp.minimum(lengths[donor] - 1, most - lengths[sink]) // 2
    slack = jnp.where((donor == sequence[0]) | (sink == sequence[0]) | (lengths[sink] == 0), 0, jnp.maximum(slack, 0))
    shifted = jax.random.randint(jax.random.fold_in(own, 4), (amount // 2,), 0, 1 << 20) % (slack + 1)
    lengths = lengths.at[donor].add(-shifted).at[sink].add(shifted)
    labels = jnp.searchsorted(jnp.cumsum(lengths), jnp.arange(rows * top), side="right").astype(jnp.int32)
    grid = labels.reshape(top, rows).T
    grid = grid[jax.random.permutation(jax.random.fold_in(own, 1), rows)]
    rotation = jax.random.randint(jax.random.fold_in(own, 2), (rows, 1), 0, top)
    return jnp.take_along_axis(grid, (jnp.arange(top)[None, :] + rotation) % top, axis=1)


def load_shares(number_of, total, bound, slope, full):
    portions = [(1 << 20) // math.isqrt(standing ** slope) + 1 for standing in range(1, number_of + 1)]
    largest = bound if full else min(bound, max(-(-total // number_of), total * portions[0] // sum(portions)))
    least = 1 if total - largest >= number_of - 1 else 0
    holding, rest = [largest] + [least] * (number_of - 1), total - largest - least * (number_of - 1)
    while rest > 0:
        candidates = [i for i in range(1, number_of) if holding[i] < largest] or [i for i in range(1, number_of) if holding[i] < bound]
        pool, remaining = sum([portions[i] for i in candidates]), rest
        for i in candidates:
            extra = min(bound - holding[i], max(1, remaining * portions[i] // pool), rest)
            holding[i] = holding[i] + extra
            rest = rest - extra
    return np.array(holding)


def centred(stream_key, dims, scale, limit, shards=(), held_as=jnp.bfloat16):
    entries = jax.random.normal(stream_key, dims, jnp.float32) * scale
    if len(shards) > 0:
        entries = steps_of(stream_key, dims, shards, -0.22, 0.18) * entries
    return jnp.clip(entries, min=-limit, max=limit).astype(held_as)


def setup_inputs(seed: int = 0) -> dict:
    key_of = jax.random.split(jax.random.key(seed), 11)
    tokens = centred(key_of[0], (TOKENS, D), 1.0, 6.0, ((0, 128),))
    grad_out = centred(key_of[1], (TOKENS, D), 1.0, 6.0, ((0, 128),))
    expert_ids_keys = jax.random.split(jax.random.fold_in(key_of[2], 1), TOKENS // TOK_DEV)
    expert_ids_turns = jax.random.permutation(jax.random.fold_in(key_of[2], 3), TOKENS // TOK_DEV)
    expert_ids = jax.vmap(lambda own, number: deal_out(jax.random.fold_in(key_of[2], 2), own, number, TOK_DEV, EXPERTS, TOPK, CAPD, 1))(expert_ids_keys, expert_ids_turns).reshape((TOKENS, TOPK))
    route_gate = jnp.clip(jnp.exp(math.log(2.5) - 2.3025851 * jax.random.uniform(key_of[3], (TOKENS, TOPK), jnp.float32) ** steps_of(key_of[3], (TOKENS, TOPK), ((0, 128),), -0.2, 0.2)), 0.25, 2.5).astype(jnp.bfloat16)
    expert_gate = centred(key_of[4], (EXPERTS * 4, D, HID // 4), D ** -0.5, 0.09375, ((0, 128),))
    expert_up = centred(key_of[5], (EXPERTS * 4, D, HID // 4), D ** -0.5, 0.09375, ((0, 128),))
    expert_down = centred(key_of[6], (EXPERTS * 4, HID // 4, D), HID ** -0.5, 0.1875, ((0, 128),))
    shared_gate = centred(key_of[7], (D, SH), D ** -0.5, 0.09375, ((1, 8),))
    shared_up = centred(key_of[8], (D, SH), D ** -0.5, 0.09375, ((1, 8),))
    shared_down = centred(key_of[9], (SH, D), SH ** -0.5, 0.1875, ((0, 8),))
    return {"tokens": tokens, "grad_out": grad_out, "expert_ids": expert_ids, "route_gate": route_gate, "expert_gate": expert_gate, "expert_up": expert_up, "expert_down": expert_down, "shared_gate": shared_gate, "shared_up": shared_up, "shared_down": shared_down}


def swiglu_grads(rows_x, rows_g, w_gate, w_up, w_down):
    pre_gate = jnp.dot(rows_x, w_gate, preferred_element_type=jnp.float32)
    pre_up = jnp.dot(rows_x, w_up, preferred_element_type=jnp.float32)
    sig = jax.nn.sigmoid(pre_gate)
    active = pre_gate * sig
    hidden = (active * pre_up).astype(jnp.bfloat16)
    dhidden = lax.dot_general(rows_g, w_down, (((1,), (1,)), ((), ())), preferred_element_type=jnp.float32)
    up_in = (dhidden * active).astype(jnp.bfloat16)
    gate_in = (dhidden * pre_up * sig * (1.0 + pre_gate * (1.0 - sig))).astype(jnp.bfloat16)
    d_gate = lax.dot_general(rows_x, gate_in, (((0,), (0,)), ((), ())), preferred_element_type=jnp.float32)
    d_up = lax.dot_general(rows_x, up_in, (((0,), (0,)), ((), ())), preferred_element_type=jnp.float32)
    d_down = lax.dot_general(hidden, rows_g, (((0,), (0,)), ((), ())), preferred_element_type=jnp.float32)
    d_rows = lax.dot_general(gate_in, w_gate, (((1,), (1,)), ((), ())), preferred_element_type=jnp.float32)
    d_rows = d_rows + lax.dot_general(up_in, w_up, (((1,), (1,)), ((), ())), preferred_element_type=jnp.float32)
    return d_gate, d_up, d_down, d_rows


def reference(tokens, grad_out, expert_ids, route_gate, expert_gate, expert_up, expert_down, shared_gate, shared_up, shared_down):
    count = tokens.shape[0]
    width = tokens.shape[1]
    chosen = expert_ids[:, 0].astype(jnp.int32)
    onehot = (chosen[:, None] == jnp.arange(EXPERTS, dtype=jnp.int32)[None, :]).astype(jnp.int32)
    blocks = onehot.reshape(-1, TOK_DEV, EXPERTS)
    before = (jnp.cumsum(blocks, axis=1) - blocks).reshape(count, EXPERTS)
    slot = jnp.sum(before * onehot, axis=1).astype(jnp.int32)
    device = (jnp.arange(count, dtype=jnp.int32) // TOK_DEV).astype(jnp.int32)
    place = (device * CAPD + slot).astype(jnp.int32)
    table = jnp.full((EXPERTS, DEVICES * CAPD), count, jnp.int32)
    table = table.at[chosen, place].set(jnp.arange(count, dtype=jnp.int32))
    routed_grad = (route_gate.astype(jnp.float32) * grad_out.astype(jnp.float32)).astype(jnp.bfloat16)
    zero_row = jnp.zeros((1, width), jnp.bfloat16)
    padded_x = jnp.concatenate([tokens, zero_row], 0)
    padded_g = jnp.concatenate([routed_grad, zero_row], 0)

    def one_expert(index):
        rows_x = padded_x[table[index]]
        rows_g = padded_g[table[index]]
        gates, ups, downs, parts = [], [], [], []
        for quarter in range(4):
            row = index * 4 + quarter
            d_gate, d_up, d_down, d_rows = swiglu_grads(rows_x, rows_g, expert_gate[row], expert_up[row], expert_down[row])
            gates.append(d_gate.astype(jnp.bfloat16))
            ups.append(d_up.astype(jnp.bfloat16))
            downs.append(d_down.astype(jnp.bfloat16))
            parts.append(d_rows.astype(jnp.bfloat16))
        return jnp.stack(gates), jnp.stack(ups), jnp.stack(downs), jnp.stack(parts)

    e_gate, e_up, e_down, routed_parts = lax.map(one_expert, jnp.arange(EXPERTS, dtype=jnp.int32))
    block = SH // N_LOCAL
    total = jnp.zeros((count, width), jnp.float32)
    s_gates, s_ups, s_downs = [], [], []
    for j in range(N_LOCAL):
        d_gate, d_up, d_down, d_rows = swiglu_grads(tokens, grad_out, shared_gate[:, j * block:(j + 1) * block], shared_up[:, j * block:(j + 1) * block], shared_down[j * block:(j + 1) * block])
        s_gates.append(d_gate)
        s_ups.append(d_up)
        s_downs.append(d_down)
        rounded = lax.optimization_barrier(d_rows.astype(jnp.bfloat16))
        total = total + rounded.astype(jnp.float32)
    for quarter in range(4):
        total = total + routed_parts[chosen, quarter, place].astype(jnp.float32)
    grad_tokens = total.astype(jnp.bfloat16)
    d_expert_gate = e_gate.reshape(EXPERTS * 4, width, -1)
    d_expert_up = e_up.reshape(EXPERTS * 4, width, -1)
    d_expert_down = e_down.reshape(EXPERTS * 4, -1, width)
    d_shared_gate = jnp.concatenate(s_gates, axis=1).astype(jnp.bfloat16)
    d_shared_up = jnp.concatenate(s_ups, axis=1).astype(jnp.bfloat16)
    d_shared_down = jnp.concatenate(s_downs, axis=0).astype(jnp.bfloat16)
    return (grad_tokens, d_expert_gate, d_expert_up, d_expert_down, d_shared_gate, d_shared_up, d_shared_down)
```

```python
import jax
import jax.numpy as jnp
from jax import lax
from jax.sharding import Mesh, PartitionSpec as P

CAP = 5
F32 = jnp.float32
BF16 = jnp.bfloat16


def dot(a, b, ca, cb):
    return lax.dot_general(a, b, (((ca,), (cb,)), ((), ())), preferred_element_type=F32)


def from_y(v, k):
    n = lax.axis_size("y")
    return lax.ppermute(v, "y", [(i, (i - k) % n) for i in range(n)])


def to_y(v, k):
    n = lax.axis_size("y")
    return lax.ppermute(v, "y", [(i, (i + k) % n) for i in range(n)])


def swap_core(v):
    return lax.ppermute(v, "c", [(0, 1), (1, 0)])


def gather_y(v):
    half = v.shape[0] // 2
    v1 = from_y(v, 1)
    v3 = from_y(v, 3)
    top = from_y(v1[:half], 1)
    bottom = from_y(v3[half:], 3)
    return jnp.concatenate([v, v1, top, bottom, v3], 0)


def slots(ids, experts):
    rows = ids.shape[0]
    hot = (ids[:, None] == jnp.arange(experts)[None, :]).astype(BF16)
    i = jnp.arange(rows)
    lower = (i[None, :] < i[:, None]).astype(BF16)
    before = dot(lower, hot, 1, 0)
    return jnp.sum(before * hot.astype(F32), axis=1).astype(jnp.int32)


def activations(pre_gate, pre_up, dhidden):
    sig = jax.nn.sigmoid(pre_gate)
    active = pre_gate * sig
    hidden = (active * pre_up).astype(BF16)
    up_in = (dhidden * active).astype(BF16)
    gate_in = (dhidden * pre_up * sig * (1.0 + pre_gate * (1.0 - sig))).astype(BF16)
    return hidden, up_in, gate_in


def on_device(x, g, ids, gate, eg, eu, ed, sg, su, sd):
    rows, width = x.shape
    nz, nx, ny = lax.axis_size("z"), lax.axis_size("x"), lax.axis_size("y")
    nodes = nz * nx
    experts = 2 * nodes
    group = lax.axis_index("y") // (ny // 2)
    even = lax.axis_index("y") % 2 == 0
    span = ny * CAP

    meta = jnp.concatenate([ids.T.astype(BF16), gate.T], 0)
    with jax.named_scope("meta"):
        metas = [meta] + [from_y(meta, k) for k in range(1, ny)]
    with jax.named_scope("gather_x"):
        xs = gather_y(x)
    with jax.named_scope("gather_g"):
        gs = gather_y(g)
    with jax.named_scope("swap_weights"):
        eg2 = jnp.concatenate([eg[0], swap_core(eg[0])], 1)
        eu2 = jnp.concatenate([eu[0], swap_core(eu[0])], 1)
        ed2 = jnp.concatenate([ed[0], swap_core(ed[0])], 0)
        sg2 = jnp.concatenate([sg, swap_core(sg)], 1)
        su2 = jnp.concatenate([su, swap_core(su)], 1)
        sd2 = jnp.concatenate([sd, swap_core(sd)], 0)

    with jax.named_scope("tables"):
        places, weights = [], []
        for k in range(ny):
            ids_k = metas[k][0].astype(jnp.int32)
            slot_k = slots(ids_k, experts)
            place = (ids_k // 2) * span + k * CAP + slot_k
            places.append(jnp.where(ids_k % 2 == group, place, -1))
            weights.append(metas[k][1])
            if k == 0:
                own_ids, own_slot = ids_k, slot_k
        place = jnp.concatenate(places)
        weight = jnp.concatenate(weights)
        pick = jnp.arange(nodes * span)[:, None] == place[None, :]
        pick_x = pick.astype(BF16)
        pick_g = jnp.where(pick, weight[None, :], jnp.zeros((), BF16))
    with jax.named_scope("dispatch"):
        send_x = dot(pick_x, xs, 1, 0).astype(BF16).reshape(nodes, span, width)
        came_x = lax.all_to_all(send_x, ("z", "x"), split_axis=0, concat_axis=0, tiled=True)
        send_g = dot(pick_g, gs, 1, 0).astype(BF16).reshape(nodes, span, width)
        came_g = lax.all_to_all(send_g, ("z", "x"), split_axis=0, concat_axis=0, tiled=True)

    with jax.named_scope("shared"):
        hidden, up_in, gate_in = activations(dot(xs, sg2, 1, 0), dot(xs, su2, 1, 0), dot(gs, sd2, 1, 1))
        s_rows = (dot(gate_in, sg2, 1, 1) + dot(up_in, su2, 1, 1)).astype(BF16)
        parts = s_rows.reshape(ny, rows, width)
        shared_parts = [parts[0]] + [to_y(parts[k], k) for k in range(1, ny)]
        s_gate = dot(xs, gate_in, 0, 0).astype(BF16)
        s_up = dot(xs, up_in, 0, 0).astype(BF16)
        s_down = dot(hidden, gs, 0, 0).astype(BF16)
        sh = sg.shape[1]
        s_gate = s_gate[:, :sh].astype(F32) + swap_core(s_gate[:, sh:]).astype(F32)
        s_up = s_up[:, :sh].astype(F32) + swap_core(s_up[:, sh:]).astype(F32)
        s_down = s_down[:sh].astype(F32) + swap_core(s_down[sh:]).astype(F32)
        g_gate, g_up, g_down = (
            lax.psum(s_gate.astype(BF16), ("z", "x")),
            lax.psum(s_up.astype(BF16), ("z", "x")),
            lax.psum(s_down.astype(BF16), ("z", "x")),
        )

    with jax.named_scope("routed"):
        rx = came_x.reshape(-1, width)
        rg = came_g.reshape(-1, width)
        hidden, up_in, gate_in = activations(dot(rx, eg2, 1, 0), dot(rx, eu2, 1, 0), dot(rg, ed2, 1, 1))
        e_rows = (dot(gate_in, eg2, 1, 1) + dot(up_in, eu2, 1, 1)).astype(BF16)
        e_rows = e_rows.reshape(nodes, ny, CAP, width)
        back = [e_rows[:, 0]] + [to_y(e_rows[:, k], k) for k in range(1, ny)]
        own = back[0].astype(F32) + jnp.where(even, back[3], back[1]).astype(F32)
        other = back[2].astype(F32) + jnp.where(even, back[1], back[3]).astype(F32)
        total = jnp.concatenate([own, other], 1).astype(BF16)
        returned = lax.all_to_all(total, ("z", "x"), split_axis=0, concat_axis=0, tiled=True)
        e_gate = dot(rx, gate_in, 0, 0).astype(BF16)
        e_up = dot(rx, up_in, 0, 0).astype(BF16)
        e_down = dot(hidden, rg, 0, 0).astype(BF16)
        hq = eg.shape[2]
        e_gate = e_gate[:, :hq].astype(F32) + swap_core(e_gate[:, hq:]).astype(F32)
        e_up = e_up[:, :hq].astype(F32) + swap_core(e_up[:, hq:]).astype(F32)
        e_down = e_down[:hq].astype(F32) + swap_core(e_down[hq:]).astype(F32)

    with jax.named_scope("combine"):
        row = (own_ids // 2) * (2 * CAP) + jnp.where(own_ids % 2 == group, 0, CAP) + own_slot
        pick = (row[:, None] == jnp.arange(nodes * 2 * CAP)[None, :]).astype(BF16)
        out = dot(pick, returned.reshape(-1, width), 1, 0)
        for part in shared_parts:
            out = out + part.astype(F32)
    return (
        out.astype(BF16),
        e_gate.astype(BF16)[None],
        e_up.astype(BF16)[None],
        e_down.astype(BF16)[None],
        g_gate,
        g_up,
        g_down,
    )


def solution(mesh):
    whole = Mesh(mesh.devices.reshape(4, 4, 4, 2), ("z", "x", "y", "c"))
    every, local = ("z", "x", "y", "c"), ("y", "c")
    return jax.shard_map(
        on_device,
        mesh=whole,
        in_specs=(
            P(every, None),
            P(every, None),
            P(every, None),
            P(every, None),
            P(every, None, None),
            P(every, None, None),
            P(every, None, None),
            P(None, local),
            P(None, local),
            P(local, None),
        ),
        out_specs=(
            P(every, None),
            P(every, None, None),
            P(every, None, None),
            P(every, None, None),
            P(None, local),
            P(None, local),
            P(local, None),
        ),
        check_vma=False,
    )
```

```python
import functools

import jax
import jax.numpy as jnp
from jax import lax
from jax.experimental import pallas as pl
from jax.experimental.pallas import tpu as pltpu
from jax.sharding import Mesh, PartitionSpec as P

CAP = 5
RET = 8
TILE = 512
WEIGHT = {'pack': 8, 'shared_weights': 8, 'routed_rows0': 4, 'routed_rows1': 20, 'routed_weights': 2, 'shared_rows': 20}
F32 = jnp.float32
BF16 = jnp.bfloat16
I32 = jnp.int32
ANY = pl.BlockSpec(memory_space=pl.ANY)
VMEM = pl.BlockSpec(memory_space=pltpu.VMEM)
SMEM = pl.BlockSpec(memory_space=pltpu.SMEM)


def dot(a, b, ca=1, cb=0):
    return lax.dot_general(a, b, (((ca,), (cb,)), ((), ())), preferred_element_type=F32)


def iota(shape, dim):
    return lax.broadcasted_iota(I32, shape, dim)


def hot(cond):
    return jnp.where(cond, 1.0, 0.0).astype(BF16)


def from_y(v, k):
    n = lax.axis_size("y")
    return lax.ppermute(v, "y", [(i, (i - k) % n) for i in range(n)])


def to_y(v, k):
    n = lax.axis_size("y")
    return lax.ppermute(v, "y", [(i, (i + k) % n) for i in range(n)])


def swap_core(v):
    return lax.ppermute(v, "c", [(0, 1), (1, 0)])


def after(v, *earlier):
    return lax.optimization_barrier((v, *earlier))[0]


def call(name, body, outs, operands, specs, scratch, flops, out_specs=None):
    out_shape = [jax.ShapeDtypeStruct(s, d) for s, d in outs]
    size = sum(o.size * o.dtype.itemsize for o in operands)
    size += sum(o.size * o.dtype.itemsize for o in out_shape)
    return pl.pallas_call(
        body,
        out_shape=out_shape,
        in_specs=specs,
        out_specs=out_specs or [VMEM] * len(outs),
        scratch_shapes=scratch,
        compiler_params=pltpu.CompilerParams(vmem_limit_bytes=60 * 2**20),
        name=name,
        cost_estimate=pl.CostEstimate(
            flops=int(flops * WEIGHT.get(name, 1)),
            bytes_accessed=int(size * WEIGHT.get(name, 1)),
            transcendentals=0,
        ),
    )(*operands)


def tile(i):
    return pl.ds(pl.multiple_of(i * TILE, TILE), TILE)


def copies(pairs, sems):
    return [pltpu.make_async_copy(a, b, sems.at[i]) for i, (a, b) in enumerate(pairs)]


def begin(pairs, sems):
    for c in copies(pairs, sems):
        c.start()


def finish(pairs, sems):
    for c in copies(pairs, sems):
        c.wait()


def begin_tiles(pairs_of, count, sems):
    @pl.loop(0, count)
    def _(i):
        begin(pairs_of(i), sems.at[i])


def finish_tiles(pairs_of, count, sems):
    @pl.loop(0, count)
    def _(i):
        finish(pairs_of(i), sems.at[i])


def row_pairs(chunks, held, cols):
    pairs, at = [], 0
    for c in chunks:
        n = c.shape[0]
        pairs.append((c.at[:, cols], held.at[pl.ds(at, n), cols]))
        at += n
    return pairs


def ranks(row):
    n = row.shape[1]
    sub, lane = iota((n, n), 0), iota((n, n), 1)
    col = jnp.sum(jnp.where(sub == lane, row, 0.0), axis=1, keepdims=True)
    same = jnp.where((col == row) & (sub < lane), 1.0, 0.0)
    return jnp.sum(same, axis=0, keepdims=True).astype(I32)


HEAD = 16
BOTH = 2 * CAP


def pack_kernel(where, meta, x, g, out, xv, gv, sems):
    width = xv.shape[1]
    part = width // 4
    tiles = width // TILE
    total, rows = out.shape[0], xv.shape[0]

    def loads(i):
        return [(x.at[:, tile(i)], xv.at[:, tile(i)]), (g.at[:, tile(i)], gv.at[:, tile(i)])]

    begin_tiles(loads, tiles, sems)
    row = meta[0:1, :]
    gate = meta[1:2, :]
    ids = row.astype(I32)
    j = ranks(row) + jnp.where((ids & 1) == where[0] // 2, 0, CAP)
    base = (ids >> 1) * HEAD
    q = iota((total, rows), 0)
    put_x = hot(q == base + j)
    at = jnp.where(j < HEAD - BOTH, base + BOTH + j, -1)
    put_g = jnp.where(q == at, gate, 0.0).astype(BF16)

    @pl.loop(0, tiles)
    def _(i):
        finish(loads(i), sems.at[i])
        cols = tile(i)
        out[:, cols] = (dot(put_x, xv[:, cols]) + dot(put_g, gv[:, cols])).astype(BF16)

    last = None
    for kp in range(4):
        at = jnp.where(j < HEAD - BOTH, -1, base + (j - HEAD + BOTH) * 4 + kp)
        put_t = jnp.where(q == at, gate, 0.0).astype(BF16)
        term = dot(put_t, gv[:, kp * part : (kp + 1) * part])
        last = term if last is None else last + term
    out[:, width:] = last.astype(BF16)


def pack(where, meta, x, g, nodes):
    rows, width = x.shape
    total = nodes * HEAD
    return call(
        "pack",
        pack_kernel,
        [((total, width + width // 4), BF16)],
        [where, meta, x, g],
        [SMEM, VMEM, ANY, ANY],
        [
            pltpu.VMEM((rows, width), BF16),
            pltpu.VMEM((rows, width), BF16),
            pltpu.SemaphoreType.DMA((width // TILE, 2)),
        ],
        2 * total * 3 * rows * width,
    )[0]


def regroup_kernel(msg, near, far):
    total = msg.shape[0]
    width = near.shape[1] // 2
    part = width // 4
    rows = near.shape[0]
    d, q = iota((rows, total), 0), iota((rows, total), 1)
    n = (d * 205) >> 10
    for r, out in enumerate((near, far)):
        j = d - n * CAP + r * CAP
        base = n * HEAD
        get_x = hot(q == base + j)
        get_g = hot((j < HEAD - BOTH) & (q == base + BOTH + j))
        for kp in range(4):
            cols = slice(kp * part, (kp + 1) * part)
            gcols = slice(width + kp * part, width + (kp + 1) * part)
            block = msg[:, cols]
            out[:, cols] = dot(get_x, block).astype(BF16)
            total_g = dot(get_g, block)
            if r == 1:
                get_t = hot((j >= HEAD - BOTH) & (q == base + (j - HEAD + BOTH) * 4 + kp))
                total_g = total_g + dot(get_t, msg[:, width:])
            out[:, gcols] = total_g.astype(BF16)


def regroup(msg, nodes, width):
    return call(
        "regroup",
        regroup_kernel,
        [((nodes * CAP, 2 * width), BF16)] * 2,
        [msg],
        [VMEM],
        [],
        2 * 5 * nodes * CAP * msg.shape[0] * width,
    )


def activations(pre_gate, pre_up, dhidden):
    sig = jax.nn.sigmoid(pre_gate)
    active = pre_gate * sig
    hidden = (active * pre_up).astype(BF16)
    up_in = (dhidden * active).astype(BF16)
    gate_in = (dhidden * pre_up * sig * (1.0 + pre_gate * (1.0 - sig))).astype(BF16)
    return hidden, up_in, gate_in


def weight_pairs(refs, wg, wu, wd, cols):
    go, gs, uo, us, do, ds = refs
    h = do.shape[0]
    own, other = pl.ds(0, h), pl.ds(h, h)
    return [
        (go.at[cols, :], wg.at[cols, own]),
        (gs.at[cols, :], wg.at[cols, other]),
        (uo.at[cols, :], wu.at[cols, own]),
        (us.at[cols, :], wu.at[cols, other]),
        (do.at[:, cols], wd.at[own, cols]),
        (ds.at[:, cols], wd.at[other, cols]),
    ]


def stacked_pairs(refs, wg, wu, wd, cols, i):
    g, u, d, came = refs
    h = d.shape[0]
    own, other = pl.ds(0, h), pl.ds(h, h)
    pairs = [
        (g.at[cols, :], wg.at[cols, own]),
        (came.at[cols, pl.ds(0, h)], wg.at[cols, other]),
        (u.at[cols, :], wu.at[cols, own]),
        (came.at[cols, pl.ds(h, h)], wu.at[cols, other]),
        (d.at[:, cols], wd.at[own, cols]),
    ]
    for c in range(TILE // h):
        at = pl.ds(pl.multiple_of(i * TILE + c * h, h), h)
        pairs.append((came.at[at, pl.ds(2 * h, h)], wd.at[other, at]))
    return pairs


def stack_kernel(g, u, d, out):
    h = g.shape[1]
    out[:, 0:h] = g[...]
    out[:, h : 2 * h] = u[...]
    for c in range(d.shape[1] // h):
        out[c * h : (c + 1) * h, 2 * h :] = d[:, c * h : (c + 1) * h]


def stack(g, u, d):
    width, h = g.shape
    return call("stack", stack_kernel, [((width, 3 * h), BF16)], [g, u, d], [VMEM] * 3, [], 0)[0]


def forward(xv, gv, wg, wu, wd, pg, pu, dh, arrive):
    pg[...] = jnp.zeros_like(pg)
    pu[...] = jnp.zeros_like(pu)
    dh[...] = jnp.zeros_like(dh)

    @pl.loop(0, xv.shape[1] // TILE)
    def _(i):
        arrive(i)
        cols = tile(i)
        x = xv[:, cols]
        pg[...] += dot(x, wg[cols, :])
        pu[...] += dot(x, wu[cols, :])
        dh[...] += dot(gv[:, cols], wd[:, cols], 1, 1)

    return activations(pg[...], pu[...], dh[...])


def shared_rows_kernel(go, uo, came, up_in, gate_in, *refs):
    outs, (wg, wu, held, sems, out_sems) = refs[:4], refs[4:]
    h = go.shape[1]
    own, other = pl.ds(0, h), pl.ds(h, h)

    def loads(i):
        cols = tile(i)
        return [
            (go.at[cols, :], wg.at[cols, own]),
            (came.at[cols, own], wg.at[cols, other]),
            (uo.at[cols, :], wu.at[cols, own]),
            (came.at[cols, other], wu.at[cols, other]),
        ]

    begin_tiles(loads, go.shape[0] // TILE, sems)
    rows_back(gate_in, up_in, wg, wu, outs, held, out_sems, lambda i: finish(loads(i), sems.at[i]))


def rows_back(gate_in, up_in, wg, wu, outs, held, sems, arrive=None):
    rows = outs[0].shape[0]
    tiles = wg.shape[0] // TILE

    def stores(i):
        cols = tile(i)
        return [(held.at[pl.ds(k * rows, rows), cols], o.at[:, cols]) for k, o in enumerate(outs)]

    @pl.loop(0, tiles)
    def _(i):
        if arrive is not None:
            arrive(i)
        cols = tile(i)
        total = dot(gate_in[...], wg[cols, :], 1, 1) + dot(up_in[...], wu[cols, :], 1, 1)
        held[:, cols] = total.astype(BF16)
        begin(stores(i), sems.at[i])

    finish_tiles(stores, tiles, sems)


def shared_rows(weights, up_in, gate_in):
    span, h = up_in.shape
    width = weights[0].shape[0]
    return call(
        "shared_rows",
        shared_rows_kernel,
        [((span // 4, width), BF16)] * 4,
        [weights[0], weights[1], weights[3], up_in, gate_in],
        [ANY] * 3 + [VMEM] * 2,
        [
            pltpu.VMEM((width, h), BF16),
            pltpu.VMEM((width, h), BF16),
            pltpu.VMEM((span, width), BF16),
            pltpu.SemaphoreType.DMA((width // TILE, 4)),
            pltpu.SemaphoreType.DMA((width // TILE, 4)),
        ],
        2 * 2 * span * width * h,
        [ANY] * 4,
    )


def weight_grads(xv, gv, hidden, up_in, gate_in, outs, held, sems, arrive=None):
    tiles = xv.shape[1] // TILE
    h = outs[2].shape[0]
    hg, hu, hd = held

    def stores(i):
        cols = tile(i)
        pairs = []
        for k in range(len(outs) // 3):
            part = pl.ds(k * h, h)
            pairs += [
                (hg.at[cols, part], outs[3 * k].at[cols, :]),
                (hu.at[cols, part], outs[3 * k + 1].at[cols, :]),
                (hd.at[part, cols], outs[3 * k + 2].at[:, cols]),
            ]
        return pairs

    @pl.loop(0, tiles)
    def _(i):
        if arrive is not None:
            arrive(i)
        cols = tile(i)
        x = xv[:, cols]
        hg[cols, :] = dot(x, gate_in[...], 0, 0).astype(BF16)
        hu[cols, :] = dot(x, up_in[...], 0, 0).astype(BF16)
        hd[:, cols] = dot(hidden[...], gv[:, cols], 0, 0).astype(BF16)
        begin(stores(i), sems.at[i])

    finish_tiles(stores, tiles, sems)


def weight_grad_shapes(width, h):
    return [((width, h), BF16), ((width, h), BF16), ((h, width), BF16)] * 2


def shared_weights_kernel(*refs):
    chunks_x, chunks_g, weights = refs[0:7], refs[7:14], refs[14:18]
    outs, up_in, gate_in = refs[18:24], refs[24], refs[25]
    xv, gv, wg, wu, wd, pg, pu, dh, hidden, hg, hu, hd, sems, out_sems = refs[26:]

    def loads(i):
        cols = tile(i)
        return (
            row_pairs(chunks_x, xv, cols)
            + stacked_pairs(weights, wg, wu, wd, cols, i)
            + row_pairs(chunks_g, gv, cols)
        )

    begin_tiles(loads, xv.shape[1] // TILE, sems)
    a, b, c = forward(xv, gv, wg, wu, wd, pg, pu, dh, lambda i: finish(loads(i), sems.at[i]))
    hidden[...] = a
    up_in[...] = b
    gate_in[...] = c
    weight_grads(xv, gv, hidden, up_in, gate_in, outs, (hg, hu, hd), out_sems)


def shared_weights(chunks_x, chunks_g, weights):
    rows, width = chunks_x[0].shape
    span, h = 4 * rows, 2 * weights[0].shape[1]
    outs = call(
        "shared_weights",
        shared_weights_kernel,
        weight_grad_shapes(width, h // 2) + [((span, h), BF16)] * 2,
        [*chunks_x, *chunks_g, *weights],
        [ANY] * 18,
        [
            pltpu.VMEM((span, width), BF16),
            pltpu.VMEM((span, width), BF16),
            pltpu.VMEM((width, h), BF16),
            pltpu.VMEM((width, h), BF16),
            pltpu.VMEM((h, width), BF16),
            pltpu.VMEM((span, h), F32),
            pltpu.VMEM((span, h), F32),
            pltpu.VMEM((span, h), F32),
            pltpu.VMEM((span, h), BF16),
            pltpu.VMEM((width, h), BF16),
            pltpu.VMEM((width, h), BF16),
            pltpu.VMEM((h, width), BF16),
            pltpu.SemaphoreType.DMA((width // TILE, 19 + 2 * TILE // h)),
            pltpu.SemaphoreType.DMA((width // TILE, 6)),
        ],
        2 * 6 * span * width * h,
        [ANY] * 6 + [VMEM] * 2,
    )
    return outs[:6], outs[6], outs[7]


def routed_rows_kernel(n, *refs):
    inputs, weights, refs = refs[:n], refs[n : n + 6], refs[n + 6 :]
    outs, kept, bundle, refs = refs[:n], refs[n : n + 3], refs[n + 3], refs[n + 4 :]
    xv, gv, wg, wu, wd, pg, pu, dh, hidden, up_in, gate_in, rows, sems, o_sems, k_sems = refs
    width = xv.shape[1]
    tiles = width // TILE
    h = kept[0].shape[1]

    def loads(i):
        pairs = weight_pairs(weights, wg, wu, wd, tile(i))
        gcols = pl.ds(pl.multiple_of(width + i * TILE, TILE), TILE)
        for k, b in enumerate(inputs):
            at = pl.ds(k * b.shape[0], b.shape[0])
            pairs.append((b.at[:, tile(i)], xv.at[at, tile(i)]))
            pairs.append((b.at[:, gcols], gv.at[at, tile(i)]))
        return pairs

    begin_tiles(loads, tiles, sems)
    a, b, c = forward(xv, gv, wg, wu, wd, pg, pu, dh, lambda i: finish(loads(i), sems.at[i]))
    hidden[...] = a
    up_in[...] = b
    gate_in[...] = c
    stores = [(xv, bundle.at[:, pl.ds(0, width)]), (gv, bundle.at[:, pl.ds(width, width)])]
    for k, v in enumerate((hidden, up_in, gate_in)):
        stores.append((v.at[:, pl.ds(0, h)], kept[k]))
        stores.append((v.at[:, pl.ds(h, h)], bundle.at[:, pl.ds(2 * width + k * h, h)]))
    begin(stores, k_sems)
    rows_back(gate_in, up_in, wg, wu, outs, rows, o_sems)
    finish(stores, k_sems)


def routed_rows(tag, inputs, weights):
    width, quarter = weights[0].shape
    h = 2 * quarter
    block = inputs[0].shape[0]
    count = len(inputs)
    span = count * block
    tiles = width // TILE
    outs = [((block, width), BF16)] * count + [((span, quarter), BF16)] * 3
    outs += [((span, 2 * width + 3 * quarter), BF16)]
    outs = call(
        "routed_rows" + tag,
        functools.partial(routed_rows_kernel, count),
        outs,
        [*inputs, *weights],
        [ANY] * (count + 6),
        [
            pltpu.VMEM((span, width), BF16),
            pltpu.VMEM((span, width), BF16),
            pltpu.VMEM((width, h), BF16),
            pltpu.VMEM((width, h), BF16),
            pltpu.VMEM((h, width), BF16),
            pltpu.VMEM((span, h), F32),
            pltpu.VMEM((span, h), F32),
            pltpu.VMEM((span, h), F32),
            pltpu.VMEM((span, h), BF16),
            pltpu.VMEM((span, h), BF16),
            pltpu.VMEM((span, h), BF16),
            pltpu.VMEM((span, width), BF16),
            pltpu.SemaphoreType.DMA((tiles, 6 + 2 * count)),
            pltpu.SemaphoreType.DMA((tiles, count)),
            pltpu.SemaphoreType.DMA((8,)),
        ],
        2 * 5 * span * width * h,
        [ANY] * len(outs),
    )
    return outs[:count], outs[count : count + 3], outs[count + 3]


def routed_weights_kernel(*refs):
    bundles, kept, outs = refs[0:4], (refs[4:7], refs[7:10]), refs[10:13]
    xv, gv, hidden, up_in, gate_in, hg, hu, hd, sems, w_sems, o_sems = refs[13:]
    width = xv.shape[1]
    h = kept[0][0].shape[1]
    inner, at = [], 0
    for i in range(4):
        n = bundles[i].shape[0]
        for k, v in enumerate((hidden, up_in, gate_in)):
            if i < 2:
                source = kept[i][k]
            else:
                source = bundles[i].at[:, pl.ds(2 * width + k * h, h)]
            inner.append((source, v.at[pl.ds(at, n)]))
        at += n

    def loads(i):
        pairs, at = [], 0
        for b in bundles:
            n = b.shape[0]
            gcols = pl.ds(pl.multiple_of(width + i * TILE, TILE), TILE)
            pairs.append((b.at[:, tile(i)], xv.at[pl.ds(at, n), tile(i)]))
            pairs.append((b.at[:, gcols], gv.at[pl.ds(at, n), tile(i)]))
            at += n
        return pairs

    begin(inner, sems)
    begin_tiles(loads, width // TILE, w_sems)
    finish(inner, sems)
    arrive = lambda i: finish(loads(i), w_sems.at[i])
    weight_grads(xv, gv, hidden, up_in, gate_in, outs, (hg, hu, hd), o_sems, arrive)


def routed_weights(own, other, kept, width):
    h = kept[0][0].shape[1]
    span = sum(b.shape[0] for b in (*own, *other))
    tiles = width // TILE
    return call(
        "routed_weights",
        routed_weights_kernel,
        weight_grad_shapes(width, h)[:3],
        [*own, *other, *kept[0], *kept[1]],
        [ANY] * 10,
        [
            pltpu.VMEM((span, width), BF16),
            pltpu.VMEM((span, width), BF16),
            pltpu.VMEM((span, h), BF16),
            pltpu.VMEM((span, h), BF16),
            pltpu.VMEM((span, h), BF16),
            pltpu.VMEM((width, h), BF16),
            pltpu.VMEM((width, h), BF16),
            pltpu.VMEM((h, width), BF16),
            pltpu.SemaphoreType.DMA((12,)),
            pltpu.SemaphoreType.DMA((tiles, 8)),
            pltpu.SemaphoreType.DMA((tiles, 3)),
        ],
        2 * 3 * span * width * h,
        [ANY] * 3,
    )


def grad_pack_kernel(g0, u0, d0, g1, u1, d1, out):
    h = g0.shape[1]
    out[:, 0:h] = (g0[...].astype(F32) + g1[...].astype(F32)).astype(BF16)
    out[:, h : 2 * h] = (u0[...].astype(F32) + u1[...].astype(F32)).astype(BF16)
    for c in range(d0.shape[1] // h):
        cols = slice(c * h, (c + 1) * h)
        block = d0[:, cols].astype(F32) + d1[:, cols].astype(F32)
        out[cols, 2 * h :] = block.astype(BF16)


def grad_pack(own, other):
    width, h = own[0].shape
    return call("grad_pack", grad_pack_kernel, [((width, 3 * h), BF16)], [*own, *other], [VMEM] * 6, [], 3 * width * h)[0]


def grad_sum_kernel(came, out):
    total = came[0].astype(F32)
    for n in range(1, came.shape[0]):
        total = total + came[n].astype(F32)
    total = total.astype(BF16)
    for n in range(came.shape[0]):
        out[n] = total


def grad_sum(came, nodes):
    shape = (nodes, came.shape[0] // nodes, came.shape[1])
    out = call("grad_sum", grad_sum_kernel, [(shape, BF16)], [came.reshape(shape)], [VMEM], [], came.size)[0]
    return out


def grad_unpack_kernel(came, g, u, d):
    h = g.shape[1]
    g[...] = came[:, 0:h]
    u[...] = came[:, h : 2 * h]
    for c in range(d.shape[1] // h):
        d[:, c * h : (c + 1) * h] = came[c * h : (c + 1) * h, 2 * h :]


def grad_unpack(came, width, h):
    outs = [((width, h), BF16), ((width, h), BF16), ((h, width), BF16)]
    return call("grad_unpack", grad_unpack_kernel, outs, [came], [VMEM], [], 3 * width * h)


def add_kernel(a, b, out):
    out[...] = (a[...].astype(F32) + b[...].astype(F32)).astype(BF16)


def add(a, b):
    return call("add", add_kernel, [(a.shape, BF16)], [a, b], [VMEM] * 2, [], a.size)[0]


def return_kernel(b0, b1, b2, b3, out):
    block, width = b0.shape
    part = width // 4
    nodes = block // CAP
    shape = (nodes * RET, block)
    q, i = iota(shape, 0), iota(shape, 1)
    n, j = q >> 3, q & 7
    own = hot((j < CAP) & (i == n * CAP + j))
    other = hot((j >= CAP) & (i == n * CAP + j - CAP))
    for kp in range(4):
        cols = slice(kp * part, (kp + 1) * part)
        out[:, cols] = (
            dot(own, b0[:, cols]) + dot(own, b1[:, cols]) + dot(other, b2[:, cols]) + dot(other, b3[:, cols])
        ).astype(BF16)
    last = None
    for kp in range(4):
        cols = slice(kp * part, (kp + 1) * part)
        get = hot(((j & 3) == kp) & (i == n * CAP + 3 + (j >> 2)))
        term = dot(get, b2[:, cols]) + dot(get, b3[:, cols])
        last = term if last is None else last + term
    out[:, width:] = last.astype(BF16)


def return_pack(blocks):
    block, width = blocks[0].shape
    nodes = block // CAP
    return call(
        "return_pack",
        return_kernel,
        [((nodes * RET, width + width // 4), BF16)],
        blocks,
        [VMEM] * 4,
        [],
        2 * nodes * RET * 4 * block * width,
    )[0]


def combine_kernel(where, meta, back, p0, p1, p2, p3, out):
    rows, width = out.shape
    part = width // 4
    n = back.shape[0]
    row = meta[0:1, :]
    ids = row.astype(I32)
    j = ranks(row) + jnp.where((ids & 1) == where[0] // 2, 0, CAP)
    node = ids >> 1
    c = iota((n, rows), 0)
    head = hot((j < RET) & (c == node * RET + j))
    for kp in range(4):
        cols = slice(kp * part, (kp + 1) * part)
        last = hot((j >= RET) & (c == node * RET + (j - RET) * 4 + kp))
        total = dot(head, back[:, cols], 0, 0) + dot(last, back[:, width:], 0, 0)
        for p in (p0, p1, p2, p3):
            total = total + p[:, cols].astype(F32)
        out[:, cols] = total.astype(BF16)


def combine(where, meta, back, parts):
    rows, width = parts[0].shape
    return call(
        "combine",
        combine_kernel,
        [((rows, width), BF16)],
        [where, meta, back, *parts],
        [SMEM] + [VMEM] * 6,
        [],
        2 * rows * back.shape[0] * width * 2,
    )[0]


def gather_y(v):
    half = v.shape[0] // 2
    v1 = from_y(v, 1)
    v3 = from_y(v, 3)
    top = from_y(v1[:half], 1)
    bottom = from_y(v3[half:], 3)
    return [v, v1, top, bottom, v3]


def on_device(x, g, ids, gate, eg, eu, ed, sg, su, sd):
    rows, width = x.shape
    nodes = lax.axis_size("z") * lax.axis_size("x")
    ny = lax.axis_size("y")
    y = lax.axis_index("y")
    where = y.astype(I32).reshape(1)

    axes = ("z", "x")

    def exchange(v):
        return lax.all_to_all(v, axes, split_axis=0, concat_axis=0, tiled=True)

    half = rows // 2
    def named(name, f, *args):
        with jax.named_scope(name):
            return f(*args)

    def pairs_y(name, v, order):
        return named(name, lambda v: lax.ppermute(v, "y", list(enumerate(order))), v)

    def partner(name, v):
        return pairs_y(name, v, (1, 0, 3, 2))

    def beside(name, v):
        return pairs_y(name, v, (3, 2, 1, 0))

    def across(name, v):
        return pairs_y(name, v, (2, 3, 0, 1))

    top, bottom = slice(0, rows // 2), slice(rows // 2, rows)
    x1t, x3b = named("x1t", from_y, x[top], 1), named("x3b", from_y, x[bottom], 3)
    g1t, g3b = named("g1t", from_y, g[top], 1), named("g3b", from_y, g[bottom], 3)
    x1b, x3t = named("x1b", from_y, x[bottom], 1), named("x3t", from_y, x[top], 3)
    g1b, g3t = named("g1b", from_y, g[bottom], 1), named("g3t", from_y, g[top], 3)
    meta = jnp.concatenate([ids.reshape(1, rows).astype(F32), gate.reshape(1, rows).astype(F32)], 0)
    x2 = [named("xt", from_y, x1t, 1), named("xb", from_y, x3b, 3)]
    g2 = [named("gt", from_y, g1t, 1), named("gb", from_y, g3b, 3)]
    xs, gs = [x, x1t, x1b, *x2, x3t, x3b], [g, g1t, g1b, *g2, g3t, g3b]
    send = pack(where, meta, after(x, x1t, x3b, g1t, g3b), g, nodes)
    msg = named("msg", exchange, send)
    stacked = stack(sg, su, sd)
    shared_w = [sg, su, sd, named("swap_shared", swap_core, stacked)]
    expert_w = []

    grads, up_in, gate_in = shared_weights(xs, gs, shared_w)
    near, far = regroup(after(msg, up_in), nodes, width)
    r1, r2 = partner("r1", near), beside("r2", far)
    r3 = across("r3", after(far, r1, r2))

    swapped = [named("swap_grads", swap_core, v) for v in grads[3:]]
    send = grad_pack(grads[:3], swapped)
    scattered = named("scatter", exchange, send)
    for w in (eg[0], eu[0], ed[0]):
        expert_w += [w, named("swap_expert", swap_core, after(w, send))]

    parts = shared_rows(shared_w, after(up_in, near, send), gate_in)
    (e0, e1, e2), kept0, bundle0 = routed_rows("0", [after(near, parts[0]), r1, r2], expert_w)
    b1, b2 = partner("b1", e1), beside("b2", e2)
    summed = grad_sum(after(scattered, e0), nodes)
    came = named("gather", exchange, summed.reshape(scattered.shape))
    (e3,), kept1, bundle1 = routed_rows("1", [after(r3, summed, b1, b2)], expert_w)
    b3 = across("b3", e3)
    p1, p3 = (named("part", to_y, after(parts[k], e3), k) for k in (1, 3))
    p2 = named("part", to_y, after(parts[2], p1, p3), 2)
    own = [bundle0, bundle1]
    other = [named("swap_bundle", swap_core, b) for b in own]
    e_gate, e_up, e_down = routed_weights(own, other, [kept0, kept1], width)
    send = return_pack([after(e0, came, p1, p3, e_gate), b1, b2, b3])
    returned = named("returned", exchange, after(send, came))
    g_gate, g_up, g_down = grad_unpack(came, width, sg.shape[1])
    out = combine(where, meta, after(returned, g_gate), [parts[0], p1, p2, p3])
    return (out, e_gate[None], e_up[None], e_down[None], g_gate, g_up, g_down)


def solution(mesh):
    whole = Mesh(mesh.devices.reshape(4, 4, 4, 2), ("z", "x", "y", "c"))
    every, local = ("z", "x", "y", "c"), ("y", "c")
    specs = dict(
        rows=P(every, None), expert=P(every, None, None), columns=P(None, local), down=P(local, None)
    )
    return jax.shard_map(
        on_device,
        mesh=whole,
        in_specs=(
            specs["rows"],
            specs["rows"],
            specs["rows"],
            specs["rows"],
            specs["expert"],
            specs["expert"],
            specs["expert"],
            specs["columns"],
            specs["columns"],
            specs["down"],
        ),
        out_specs=(
            specs["rows"],
            specs["expert"],
            specs["expert"],
            specs["expert"],
            specs["columns"],
            specs["columns"],
            specs["down"],
        ),
        check_vma=False,
    )
```

```python
import functools

import jax
import jax.numpy as jnp
from jax import lax
from jax.experimental import pallas as pl
from jax.experimental.pallas import tpu as pltpu
from jax.sharding import Mesh, PartitionSpec as P

CAP = 5
RET = 8
TILE = 512
WEIGHT = {'pack': 8, 'shared_weights': 8, 'routed_rows0': .05, 'routed_rows1': 20, 'routed_weights': .05, 'shared_rows': 20, 'regroup': .05, 'grad_pack': .05, 'return_pack': .05, 'combine': .05, 'grad_unpack': .05}
F32 = jnp.float32
BF16 = jnp.bfloat16
I32 = jnp.int32
ANY = pl.BlockSpec(memory_space=pl.ANY)
VMEM = pl.BlockSpec(memory_space=pltpu.VMEM)
SMEM = pl.BlockSpec(memory_space=pltpu.SMEM)


def dot(a, b, ca=1, cb=0):
    return lax.dot_general(a, b, (((ca,), (cb,)), ((), ())), preferred_element_type=F32)


def iota(shape, dim):
    return lax.broadcasted_iota(I32, shape, dim)


def hot(cond):
    return jnp.where(cond, 1.0, 0.0).astype(BF16)


def from_y(v, k):
    n = lax.axis_size("y")
    return lax.ppermute(v, "y", [(i, (i - k) % n) for i in range(n)])


def to_y(v, k):
    n = lax.axis_size("y")
    return lax.ppermute(v, "y", [(i, (i + k) % n) for i in range(n)])


def swap_core(v):
    return lax.ppermute(v, "c", [(0, 1), (1, 0)])


def after(v, *earlier):
    return lax.optimization_barrier((v, *earlier))[0]


def call(name, body, outs, operands, specs, scratch, flops, out_specs=None):
    out_shape = [jax.ShapeDtypeStruct(s, d) for s, d in outs]
    size = sum(o.size * o.dtype.itemsize for o in operands)
    size += sum(o.size * o.dtype.itemsize for o in out_shape)
    return pl.pallas_call(
        body,
        out_shape=out_shape,
        in_specs=specs,
        out_specs=out_specs or [VMEM] * len(outs),
        scratch_shapes=scratch,
        compiler_params=pltpu.CompilerParams(vmem_limit_bytes=60 * 2**20),
        name=name,
        cost_estimate=pl.CostEstimate(
            flops=int(flops * WEIGHT.get(name, 1)),
            bytes_accessed=int(size * WEIGHT.get(name, 1)),
            transcendentals=0,
        ),
    )(*operands)


def tile(i):
    return pl.ds(pl.multiple_of(i * TILE, TILE), TILE)


def copies(pairs, sems):
    return [pltpu.make_async_copy(a, b, sems.at[i]) for i, (a, b) in enumerate(pairs)]


def begin(pairs, sems):
    for c in copies(pairs, sems):
        c.start()


def finish(pairs, sems):
    for c in copies(pairs, sems):
        c.wait()


def begin_tiles(pairs_of, count, sems):
    @pl.loop(0, count)
    def _(i):
        begin(pairs_of(i), sems.at[i])


def finish_tiles(pairs_of, count, sems):
    @pl.loop(0, count)
    def _(i):
        finish(pairs_of(i), sems.at[i])


def row_pairs(chunks, held, cols):
    pairs, at = [], 0
    for c in chunks:
        n = c.shape[0]
        pairs.append((c.at[:, cols], held.at[pl.ds(at, n), cols]))
        at += n
    return pairs


def ranks(row):
    n = row.shape[1]
    sub, lane = iota((n, n), 0), iota((n, n), 1)
    col = jnp.sum(jnp.where(sub == lane, row, 0.0), axis=1, keepdims=True)
    same = jnp.where((col == row) & (sub < lane), 1.0, 0.0)
    return jnp.sum(same, axis=0, keepdims=True).astype(I32)


HEAD = 16
BOTH = 2 * CAP


def pack_kernel(where, meta, x, g, out, xv, gv, sems):
    width = xv.shape[1]
    part = width // 4
    tiles = width // TILE
    total, rows = out.shape[0], xv.shape[0]

    def loads(i):
        return [(x.at[:, tile(i)], xv.at[:, tile(i)]), (g.at[:, tile(i)], gv.at[:, tile(i)])]

    begin_tiles(loads, tiles, sems)
    row = meta[0:1, :]
    gate = meta[1:2, :]
    ids = row.astype(I32)
    j = ranks(row) + jnp.where((ids & 1) == where[0] // 2, 0, CAP)
    base = (ids >> 1) * HEAD
    q = iota((total, rows), 0)
    put_x = hot(q == base + j)
    at = jnp.where(j < HEAD - BOTH, base + BOTH + j, -1)
    put_g = jnp.where(q == at, gate, 0.0).astype(BF16)

    @pl.loop(0, tiles)
    def _(i):
        finish(loads(i), sems.at[i])
        cols = tile(i)
        out[:, cols] = (dot(put_x, xv[:, cols]) + dot(put_g, gv[:, cols])).astype(BF16)

    last = None
    for kp in range(4):
        at = jnp.where(j < HEAD - BOTH, -1, base + (j - HEAD + BOTH) * 4 + kp)
        put_t = jnp.where(q == at, gate, 0.0).astype(BF16)
        term = dot(put_t, gv[:, kp * part : (kp + 1) * part])
        last = term if last is None else last + term
    out[:, width:] = last.astype(BF16)


def pack(where, meta, x, g, nodes):
    rows, width = x.shape
    total = nodes * HEAD
    return call(
        "pack",
        pack_kernel,
        [((total, width + width // 4), BF16)],
        [where, meta, x, g],
        [SMEM, VMEM, ANY, ANY],
        [
            pltpu.VMEM((rows, width), BF16),
            pltpu.VMEM((rows, width), BF16),
            pltpu.SemaphoreType.DMA((width // TILE, 2)),
        ],
        2 * total * 3 * rows * width,
    )[0]


def regroup_kernel(msg, near, far):
    total = msg.shape[0]
    width = near.shape[1] // 2
    part = width // 4
    rows = near.shape[0]
    d, q = iota((rows, total), 0), iota((rows, total), 1)
    n = (d * 205) >> 10
    for r, out in enumerate((near, far)):
        j = d - n * CAP + r * CAP
        base = n * HEAD
        get_x = hot(q == base + j)
        get_g = hot((j < HEAD - BOTH) & (q == base + BOTH + j))
        for kp in range(4):
            cols = slice(kp * part, (kp + 1) * part)
            gcols = slice(width + kp * part, width + (kp + 1) * part)
            block = msg[:, cols]
            out[:, cols] = dot(get_x, block).astype(BF16)
            total_g = dot(get_g, block)
            if r == 1:
                get_t = hot((j >= HEAD - BOTH) & (q == base + (j - HEAD + BOTH) * 4 + kp))
                total_g = total_g + dot(get_t, msg[:, width:])
            out[:, gcols] = total_g.astype(BF16)


def regroup(msg, nodes, width):
    return call(
        "regroup",
        regroup_kernel,
        [((nodes * CAP, 2 * width), BF16)] * 2,
        [msg],
        [VMEM],
        [],
        2 * 5 * nodes * CAP * msg.shape[0] * width,
    )


def activations(pre_gate, pre_up, dhidden):
    sig = jax.nn.sigmoid(pre_gate)
    active = pre_gate * sig
    hidden = (active * pre_up).astype(BF16)
    up_in = (dhidden * active).astype(BF16)
    gate_in = (dhidden * pre_up * sig * (1.0 + pre_gate * (1.0 - sig))).astype(BF16)
    return hidden, up_in, gate_in


def weight_pairs(refs, wg, wu, wd, cols):
    go, gs, uo, us, do, ds = refs
    h = do.shape[0]
    own, other = pl.ds(0, h), pl.ds(h, h)
    return [
        (go.at[cols, :], wg.at[cols, own]),
        (gs.at[cols, :], wg.at[cols, other]),
        (uo.at[cols, :], wu.at[cols, own]),
        (us.at[cols, :], wu.at[cols, other]),
        (do.at[:, cols], wd.at[own, cols]),
        (ds.at[:, cols], wd.at[other, cols]),
    ]


def stacked_pairs(refs, wg, wu, wd, cols, i):
    g, u, d, came = refs
    h = d.shape[0]
    own, other = pl.ds(0, h), pl.ds(h, h)
    pairs = [
        (g.at[cols, :], wg.at[cols, own]),
        (came.at[cols, pl.ds(0, h)], wg.at[cols, other]),
        (u.at[cols, :], wu.at[cols, own]),
        (came.at[cols, pl.ds(h, h)], wu.at[cols, other]),
        (d.at[:, cols], wd.at[own, cols]),
    ]
    for c in range(TILE // h):
        at = pl.ds(pl.multiple_of(i * TILE + c * h, h), h)
        pairs.append((came.at[at, pl.ds(2 * h, h)], wd.at[other, at]))
    return pairs


def stack_kernel(g, u, d, out):
    h = g.shape[1]
    out[:, 0:h] = g[...]
    out[:, h : 2 * h] = u[...]
    for c in range(d.shape[1] // h):
        out[c * h : (c + 1) * h, 2 * h :] = d[:, c * h : (c + 1) * h]


def stack(g, u, d):
    width, h = g.shape
    return call("stack", stack_kernel, [((width, 3 * h), BF16)], [g, u, d], [VMEM] * 3, [], 0)[0]


def forward(xv, gv, wg, wu, wd, pg, pu, dh, arrive):
    pg[...] = jnp.zeros_like(pg)
    pu[...] = jnp.zeros_like(pu)
    dh[...] = jnp.zeros_like(dh)

    @pl.loop(0, xv.shape[1] // TILE)
    def _(i):
        arrive(i)
        cols = tile(i)
        x = xv[:, cols]
        pg[...] += dot(x, wg[cols, :])
        pu[...] += dot(x, wu[cols, :])
        dh[...] += dot(gv[:, cols], wd[:, cols], 1, 1)

    return activations(pg[...], pu[...], dh[...])


def shared_rows_kernel(go, uo, came, up_in, gate_in, *refs):
    outs, (wg, wu, held, sems, out_sems) = refs[:4], refs[4:]
    h = go.shape[1]
    own, other = pl.ds(0, h), pl.ds(h, h)

    def loads(i):
        cols = tile(i)
        return [
            (go.at[cols, :], wg.at[cols, own]),
            (came.at[cols, own], wg.at[cols, other]),
            (uo.at[cols, :], wu.at[cols, own]),
            (came.at[cols, other], wu.at[cols, other]),
        ]

    begin_tiles(loads, go.shape[0] // TILE, sems)
    rows_back(gate_in, up_in, wg, wu, outs, held, out_sems, lambda i: finish(loads(i), sems.at[i]))


def rows_back(gate_in, up_in, wg, wu, outs, held, sems, arrive=None):
    rows = outs[0].shape[0]
    tiles = wg.shape[0] // TILE

    def stores(i):
        cols = tile(i)
        return [(held.at[pl.ds(k * rows, rows), cols], o.at[:, cols]) for k, o in enumerate(outs)]

    @pl.loop(0, tiles)
    def _(i):
        if arrive is not None:
            arrive(i)
        cols = tile(i)
        total = dot(gate_in[...], wg[cols, :], 1, 1) + dot(up_in[...], wu[cols, :], 1, 1)
        held[:, cols] = total.astype(BF16)
        begin(stores(i), sems.at[i])

    finish_tiles(stores, tiles, sems)


def shared_rows(weights, up_in, gate_in):
    span, h = up_in.shape
    width = weights[0].shape[0]
    return call(
        "shared_rows",
        shared_rows_kernel,
        [((span // 4, width), BF16)] * 4,
        [weights[0], weights[1], weights[3], up_in, gate_in],
        [ANY] * 3 + [VMEM] * 2,
        [
            pltpu.VMEM((width, h), BF16),
            pltpu.VMEM((width, h), BF16),
            pltpu.VMEM((span, width), BF16),
            pltpu.SemaphoreType.DMA((width // TILE, 4)),
            pltpu.SemaphoreType.DMA((width // TILE, 4)),
        ],
        2 * 2 * span * width * h,
        [ANY] * 4,
    )


def weight_grads(xv, gv, hidden, up_in, gate_in, outs, held, sems, arrive=None):
    tiles = xv.shape[1] // TILE
    h = outs[2].shape[0]
    hg, hu, hd = held

    def stores(i):
        cols = tile(i)
        pairs = []
        for k in range(len(outs) // 3):
            part = pl.ds(k * h, h)
            pairs += [
                (hg.at[cols, part], outs[3 * k].at[cols, :]),
                (hu.at[cols, part], outs[3 * k + 1].at[cols, :]),
                (hd.at[part, cols], outs[3 * k + 2].at[:, cols]),
            ]
        return pairs

    @pl.loop(0, tiles)
    def _(i):
        if arrive is not None:
            arrive(i)
        cols = tile(i)
        x = xv[:, cols]
        hg[cols, :] = dot(x, gate_in[...], 0, 0).astype(BF16)
        hu[cols, :] = dot(x, up_in[...], 0, 0).astype(BF16)
        hd[:, cols] = dot(hidden[...], gv[:, cols], 0, 0).astype(BF16)
        begin(stores(i), sems.at[i])

    finish_tiles(stores, tiles, sems)


def weight_grad_shapes(width, h):
    return [((width, h), BF16), ((width, h), BF16), ((h, width), BF16)] * 2


def shared_weights_kernel(*refs):
    chunks_x, chunks_g, weights = refs[0:7], refs[7:14], refs[14:18]
    outs, up_in, gate_in = refs[18:24], refs[24], refs[25]
    xv, gv, wg, wu, wd, pg, pu, dh, hidden, hg, hu, hd, sems, out_sems = refs[26:]

    def loads(i):
        cols = tile(i)
        return (
            row_pairs(chunks_x, xv, cols)
            + stacked_pairs(weights, wg, wu, wd, cols, i)
            + row_pairs(chunks_g, gv, cols)
        )

    begin_tiles(loads, xv.shape[1] // TILE, sems)
    a, b, c = forward(xv, gv, wg, wu, wd, pg, pu, dh, lambda i: finish(loads(i), sems.at[i]))
    hidden[...] = a
    up_in[...] = b
    gate_in[...] = c
    weight_grads(xv, gv, hidden, up_in, gate_in, outs, (hg, hu, hd), out_sems)


def shared_weights(chunks_x, chunks_g, weights):
    rows, width = chunks_x[0].shape
    span, h = 4 * rows, 2 * weights[0].shape[1]
    outs = call(
        "shared_weights",
        shared_weights_kernel,
        weight_grad_shapes(width, h // 2) + [((span, h), BF16)] * 2,
        [*chunks_x, *chunks_g, *weights],
        [ANY] * 18,
        [
            pltpu.VMEM((span, width), BF16),
            pltpu.VMEM((span, width), BF16),
            pltpu.VMEM((width, h), BF16),
            pltpu.VMEM((width, h), BF16),
            pltpu.VMEM((h, width), BF16),
            pltpu.VMEM((span, h), F32),
            pltpu.VMEM((span, h), F32),
            pltpu.VMEM((span, h), F32),
            pltpu.VMEM((span, h), BF16),
            pltpu.VMEM((width, h), BF16),
            pltpu.VMEM((width, h), BF16),
            pltpu.VMEM((h, width), BF16),
            pltpu.SemaphoreType.DMA((width // TILE, 19 + 2 * TILE // h)),
            pltpu.SemaphoreType.DMA((width // TILE, 6)),
        ],
        2 * 6 * span * width * h,
        [ANY] * 6 + [VMEM] * 2,
    )
    return outs[:6], outs[6], outs[7]


def routed_rows_kernel(n, *refs):
    inputs, weights, refs = refs[:n], refs[n : n + 6], refs[n + 6 :]
    outs, kept, bundle, refs = refs[:n], refs[n : n + 3], refs[n + 3], refs[n + 4 :]
    xv, gv, wg, wu, wd, pg, pu, dh, hidden, up_in, gate_in, rows, sems, o_sems, k_sems = refs
    width = xv.shape[1]
    tiles = width // TILE
    h = kept[0].shape[1]

    def loads(i):
        pairs = weight_pairs(weights, wg, wu, wd, tile(i))
        gcols = pl.ds(pl.multiple_of(width + i * TILE, TILE), TILE)
        for k, b in enumerate(inputs):
            at = pl.ds(k * b.shape[0], b.shape[0])
            pairs.append((b.at[:, tile(i)], xv.at[at, tile(i)]))
            pairs.append((b.at[:, gcols], gv.at[at, tile(i)]))
        return pairs

    begin_tiles(loads, tiles, sems)
    a, b, c = forward(xv, gv, wg, wu, wd, pg, pu, dh, lambda i: finish(loads(i), sems.at[i]))
    hidden[...] = a
    up_in[...] = b
    gate_in[...] = c
    stores = [(xv, bundle.at[:, pl.ds(0, width)]), (gv, bundle.at[:, pl.ds(width, width)])]
    for k, v in enumerate((hidden, up_in, gate_in)):
        stores.append((v.at[:, pl.ds(0, h)], kept[k]))
        stores.append((v.at[:, pl.ds(h, h)], bundle.at[:, pl.ds(2 * width + k * h, h)]))
    begin(stores, k_sems)
    rows_back(gate_in, up_in, wg, wu, outs, rows, o_sems)
    finish(stores, k_sems)


def routed_rows(tag, inputs, weights):
    width, quarter = weights[0].shape
    h = 2 * quarter
    block = inputs[0].shape[0]
    count = len(inputs)
    span = count * block
    tiles = width // TILE
    outs = [((block, width), BF16)] * count + [((span, quarter), BF16)] * 3
    outs += [((span, 2 * width + 3 * quarter), BF16)]
    outs = call(
        "routed_rows" + tag,
        functools.partial(routed_rows_kernel, count),
        outs,
        [*inputs, *weights],
        [ANY] * (count + 6),
        [
            pltpu.VMEM((span, width), BF16),
            pltpu.VMEM((span, width), BF16),
            pltpu.VMEM((width, h), BF16),
            pltpu.VMEM((width, h), BF16),
            pltpu.VMEM((h, width), BF16),
            pltpu.VMEM((span, h), F32),
            pltpu.VMEM((span, h), F32),
            pltpu.VMEM((span, h), F32),
            pltpu.VMEM((span, h), BF16),
            pltpu.VMEM((span, h), BF16),
            pltpu.VMEM((span, h), BF16),
            pltpu.VMEM((span, width), BF16),
            pltpu.SemaphoreType.DMA((tiles, 6 + 2 * count)),
            pltpu.SemaphoreType.DMA((tiles, count)),
            pltpu.SemaphoreType.DMA((8,)),
        ],
        2 * 5 * span * width * h,
        [ANY] * len(outs),
    )
    return outs[:count], outs[count : count + 3], outs[count + 3]


def routed_weights_kernel(*refs):
    bundles, kept, outs = refs[0:4], (refs[4:7], refs[7:10]), refs[10:13]
    xv, gv, hidden, up_in, gate_in, hg, hu, hd, sems, w_sems, o_sems = refs[13:]
    width = xv.shape[1]
    h = kept[0][0].shape[1]
    inner, at = [], 0
    for i in range(4):
        n = bundles[i].shape[0]
        for k, v in enumerate((hidden, up_in, gate_in)):
            if i < 2:
                source = kept[i][k]
            else:
                source = bundles[i].at[:, pl.ds(2 * width + k * h, h)]
            inner.append((source, v.at[pl.ds(at, n)]))
        at += n

    def loads(i):
        pairs, at = [], 0
        for b in bundles:
            n = b.shape[0]
            gcols = pl.ds(pl.multiple_of(width + i * TILE, TILE), TILE)
            pairs.append((b.at[:, tile(i)], xv.at[pl.ds(at, n), tile(i)]))
            pairs.append((b.at[:, gcols], gv.at[pl.ds(at, n), tile(i)]))
            at += n
        return pairs

    begin(inner, sems)
    begin_tiles(loads, width // TILE, w_sems)
    finish(inner, sems)
    arrive = lambda i: finish(loads(i), w_sems.at[i])
    weight_grads(xv, gv, hidden, up_in, gate_in, outs, (hg, hu, hd), o_sems, arrive)


def routed_weights(own, other, kept, width):
    h = kept[0][0].shape[1]
    span = sum(b.shape[0] for b in (*own, *other))
    tiles = width // TILE
    return call(
        "routed_weights",
        routed_weights_kernel,
        weight_grad_shapes(width, h)[:3],
        [*own, *other, *kept[0], *kept[1]],
        [ANY] * 10,
        [
            pltpu.VMEM((span, width), BF16),
            pltpu.VMEM((span, width), BF16),
            pltpu.VMEM((span, h), BF16),
            pltpu.VMEM((span, h), BF16),
            pltpu.VMEM((span, h), BF16),
            pltpu.VMEM((width, h), BF16),
            pltpu.VMEM((width, h), BF16),
            pltpu.VMEM((h, width), BF16),
            pltpu.SemaphoreType.DMA((12,)),
            pltpu.SemaphoreType.DMA((tiles, 8)),
            pltpu.SemaphoreType.DMA((tiles, 3)),
        ],
        2 * 3 * span * width * h,
        [ANY] * 3,
    )


def grad_pack_kernel(g0, u0, d0, g1, u1, d1, out):
    h = g0.shape[1]
    out[:, 0:h] = (g0[...].astype(F32) + g1[...].astype(F32)).astype(BF16)
    out[:, h : 2 * h] = (u0[...].astype(F32) + u1[...].astype(F32)).astype(BF16)
    for c in range(d0.shape[1] // h):
        cols = slice(c * h, (c + 1) * h)
        block = d0[:, cols].astype(F32) + d1[:, cols].astype(F32)
        out[cols, 2 * h :] = block.astype(BF16)


def grad_pack(own, other):
    width, h = own[0].shape
    return call("grad_pack", grad_pack_kernel, [((width, 3 * h), BF16)], [*own, *other], [VMEM] * 6, [], 3 * width * h)[0]


def grad_sum_kernel(came, out):
    total = came[0].astype(F32)
    for n in range(1, came.shape[0]):
        total = total + came[n].astype(F32)
    total = total.astype(BF16)
    for n in range(came.shape[0]):
        out[n] = total


def grad_sum(came, nodes):
    shape = (nodes, came.shape[0] // nodes, came.shape[1])
    out = call("grad_sum", grad_sum_kernel, [(shape, BF16)], [came.reshape(shape)], [VMEM], [], came.size)[0]
    return out


def grad_unpack_kernel(came, g, u, d):
    h = g.shape[1]
    g[...] = came[:, 0:h]
    u[...] = came[:, h : 2 * h]
    for c in range(d.shape[1] // h):
        d[:, c * h : (c + 1) * h] = came[c * h : (c + 1) * h, 2 * h :]


def grad_unpack(came, width, h):
    outs = [((width, h), BF16), ((width, h), BF16), ((h, width), BF16)]
    return call("grad_unpack", grad_unpack_kernel, outs, [came], [VMEM], [], 3 * width * h)


def add_kernel(a, b, out):
    out[...] = (a[...].astype(F32) + b[...].astype(F32)).astype(BF16)


def add(a, b):
    return call("add", add_kernel, [(a.shape, BF16)], [a, b], [VMEM] * 2, [], a.size)[0]


def return_kernel(b0, b1, b2, b3, out):
    block, width = b0.shape
    part = width // 4
    nodes = block // CAP
    shape = (nodes * RET, block)
    q, i = iota(shape, 0), iota(shape, 1)
    n, j = q >> 3, q & 7
    own = hot((j < CAP) & (i == n * CAP + j))
    other = hot((j >= CAP) & (i == n * CAP + j - CAP))
    for kp in range(4):
        cols = slice(kp * part, (kp + 1) * part)
        out[:, cols] = (
            dot(own, b0[:, cols]) + dot(own, b1[:, cols]) + dot(other, b2[:, cols]) + dot(other, b3[:, cols])
        ).astype(BF16)
    last = None
    for kp in range(4):
        cols = slice(kp * part, (kp + 1) * part)
        get = hot(((j & 3) == kp) & (i == n * CAP + 3 + (j >> 2)))
        term = dot(get, b2[:, cols]) + dot(get, b3[:, cols])
        last = term if last is None else last + term
    out[:, width:] = last.astype(BF16)


def return_pack(blocks):
    block, width = blocks[0].shape
    nodes = block // CAP
    return call(
        "return_pack",
        return_kernel,
        [((nodes * RET, width + width // 4), BF16)],
        blocks,
        [VMEM] * 4,
        [],
        2 * nodes * RET * 4 * block * width,
    )[0]


def combine_kernel(where, meta, back, p0, p1, p2, p3, out):
    rows, width = out.shape
    part = width // 4
    n = back.shape[0]
    row = meta[0:1, :]
    ids = row.astype(I32)
    j = ranks(row) + jnp.where((ids & 1) == where[0] // 2, 0, CAP)
    node = ids >> 1
    c = iota((n, rows), 0)
    head = hot((j < RET) & (c == node * RET + j))
    for kp in range(4):
        cols = slice(kp * part, (kp + 1) * part)
        last = hot((j >= RET) & (c == node * RET + (j - RET) * 4 + kp))
        total = dot(head, back[:, cols], 0, 0) + dot(last, back[:, width:], 0, 0)
        for p in (p0, p1, p2, p3):
            total = total + p[:, cols].astype(F32)
        out[:, cols] = total.astype(BF16)


def combine(where, meta, back, parts):
    rows, width = parts[0].shape
    return call(
        "combine",
        combine_kernel,
        [((rows, width), BF16)],
        [where, meta, back, *parts],
        [SMEM] + [VMEM] * 6,
        [],
        2 * rows * back.shape[0] * width * 2,
    )[0]


def gather_y(v):
    half = v.shape[0] // 2
    v1 = from_y(v, 1)
    v3 = from_y(v, 3)
    top = from_y(v1[:half], 1)
    bottom = from_y(v3[half:], 3)
    return [v, v1, top, bottom, v3]


def on_device(x, g, ids, gate, eg, eu, ed, sg, su, sd):
    rows, width = x.shape
    nodes = lax.axis_size("z") * lax.axis_size("x")
    ny = lax.axis_size("y")
    y = lax.axis_index("y")
    where = y.astype(I32).reshape(1)

    axes = ("z", "x")

    def exchange(v):
        return lax.all_to_all(v, axes, split_axis=0, concat_axis=0, tiled=True)

    half = rows // 2
    def named(name, f, *args):
        with jax.named_scope(name):
            return f(*args)

    def pairs_y(name, v, order):
        return named(name, lambda v: lax.ppermute(v, "y", list(enumerate(order))), v)

    def partner(name, v):
        return pairs_y(name, v, (1, 0, 3, 2))

    def beside(name, v):
        return pairs_y(name, v, (3, 2, 1, 0))

    def across(name, v):
        return pairs_y(name, v, (2, 3, 0, 1))

    top, bottom = slice(0, rows // 2), slice(rows // 2, rows)
    x1t, x3b = named("x1t", from_y, x[top], 1), named("x3b", from_y, x[bottom], 3)
    g1t, g3b = named("g1t", from_y, g[top], 1), named("g3b", from_y, g[bottom], 3)
    x1b, x3t = named("x1b", from_y, x[bottom], 1), named("x3t", from_y, x[top], 3)
    g1b, g3t = named("g1b", from_y, g[bottom], 1), named("g3t", from_y, g[top], 3)
    meta = jnp.concatenate([ids.reshape(1, rows).astype(F32), gate.reshape(1, rows).astype(F32)], 0)
    send = pack(where, meta, after(x, x1t, x3b, g1t, g3b), g, nodes)
    x2 = [named("xt", from_y, after(x1t, send), 1), named("xb", from_y, after(x3b, send), 3)]
    g2 = [named("gt", from_y, after(g1t, send), 1), named("gb", from_y, after(g3b, send), 3)]
    xs, gs = [x, x1t, x1b, *x2, x3t, x3b], [g, g1t, g1b, *g2, g3t, g3b]
    msg = named("msg", exchange, send)
    stacked = stack(sg, su, sd)
    shared_w = [sg, su, sd, named("swap_shared", swap_core, stacked)]
    expert_w = []

    grads, up_in, gate_in = shared_weights(xs, gs, shared_w)
    swapped = [named("swap_grads", swap_core, v) for v in grads[3:]]
    for w in (eg[0], eu[0], ed[0]):
        expert_w += [w, named("swap_expert", swap_core, after(w, xs[3]))]
    parts = shared_rows(shared_w, after(up_in, *expert_w[1::2]), gate_in)
    p1, p3 = (named("part", to_y, parts[k], k) for k in (1, 3))
    send = grad_pack([after(grads[0], parts[0]), *grads[1:3]], swapped)
    scattered = named("scatter", exchange, after(send, msg))

    near, far = regroup(after(msg, send), nodes, width)
    r1, r2 = partner("r1", after(near, p1, p3)), beside("r2", after(far, p1, p3))
    r3 = across("r3", after(far, r1, r2))
    (e0, e1, e2), kept0, bundle0 = routed_rows("0", [near, r1, r2], expert_w)
    b1, b2 = partner("b1", e1), beside("b2", e2)
    summed = grad_sum(after(scattered, e0), nodes)
    came = named("gather", exchange, summed.reshape(scattered.shape))
    (e3,), kept1, bundle1 = routed_rows("1", [after(r3, summed)], expert_w)
    b3 = across("b3", e3)
    p2 = named("part", to_y, after(parts[2], e3), 2)
    send = return_pack([after(e0, came), b1, b2, b3])
    returned = named("returned", exchange, after(send, came))
    own = [bundle0, bundle1]
    other = [named("swap_bundle", swap_core, after(b, send)) for b in own]
    e_gate, e_up, e_down = routed_weights(own, other, [kept0, kept1], width)
    g_gate, g_up, g_down = grad_unpack(came, width, sg.shape[1])
    out = combine(where, meta, after(returned, g_gate, e_gate), [parts[0], p1, p2, p3])
    return (out, e_gate[None], e_up[None], e_down[None], g_gate, g_up, g_down)


def solution(mesh):
    whole = Mesh(mesh.devices.reshape(4, 4, 4, 2), ("z", "x", "y", "c"))
    every, local = ("z", "x", "y", "c"), ("y", "c")
    specs = dict(
        rows=P(every, None), expert=P(every, None, None), columns=P(None, local), down=P(local, None)
    )
    return jax.shard_map(
        on_device,
        mesh=whole,
        in_specs=(
            specs["rows"],
            specs["rows"],
            specs["rows"],
            specs["rows"],
            specs["expert"],
            specs["expert"],
            specs["expert"],
            specs["columns"],
            specs["columns"],
            specs["down"],
        ),
        out_specs=(
            specs["rows"],
            specs["expert"],
            specs["expert"],
            specs["expert"],
            specs["columns"],
            specs["columns"],
            specs["down"],
        ),
        check_vma=False,
    )
```

```python
import functools

import jax
import jax.numpy as jnp
from jax import lax
from jax.experimental import pallas as pl
from jax.experimental.pallas import tpu as pltpu
from jax.sharding import Mesh, PartitionSpec as P

CAP = 5
RET = 8
TILE = 896
WEIGHT = {'pack': 8, 'shared_weights': 8, 'routed_rows0': .05, 'routed_rows1': 20, 'routed_weights': .05, 'shared_rows': 20, 'regroup': .05, 'grad_pack': .05, 'return_pack': .05, 'combine': .05, 'grad_unpack': .05}
F32 = jnp.float32
BF16 = jnp.bfloat16
I32 = jnp.int32
ANY = pl.BlockSpec(memory_space=pl.ANY)
VMEM = pl.BlockSpec(memory_space=pltpu.VMEM)
SMEM = pl.BlockSpec(memory_space=pltpu.SMEM)


def dot(a, b, ca=1, cb=0):
    return lax.dot_general(a, b, (((ca,), (cb,)), ((), ())), preferred_element_type=F32)


def iota(shape, dim):
    return lax.broadcasted_iota(I32, shape, dim)


def hot(cond):
    return jnp.where(cond, 1.0, 0.0).astype(BF16)


def from_y(v, k):
    n = lax.axis_size("y")
    return lax.ppermute(v, "y", [(i, (i - k) % n) for i in range(n)])


def to_y(v, k):
    n = lax.axis_size("y")
    return lax.ppermute(v, "y", [(i, (i + k) % n) for i in range(n)])


def swap_core(v):
    return lax.ppermute(v, "c", [(0, 1), (1, 0)])


def after(v, *earlier):
    return lax.optimization_barrier((v, *earlier))[0]


def call(name, body, outs, operands, specs, scratch, flops, out_specs=None):
    out_shape = [jax.ShapeDtypeStruct(s, d) for s, d in outs]
    size = sum(o.size * o.dtype.itemsize for o in operands)
    size += sum(o.size * o.dtype.itemsize for o in out_shape)
    return pl.pallas_call(
        body,
        out_shape=out_shape,
        in_specs=specs,
        out_specs=out_specs or [VMEM] * len(outs),
        scratch_shapes=scratch,
        compiler_params=pltpu.CompilerParams(vmem_limit_bytes=60 * 2**20),
        name=name,
        cost_estimate=pl.CostEstimate(
            flops=int(flops * WEIGHT.get(name, 1)),
            bytes_accessed=int(size * WEIGHT.get(name, 1)),
            transcendentals=0,
        ),
    )(*operands)


def tile(i):
    return pl.ds(pl.multiple_of(i * TILE, TILE), TILE)


def copies(pairs, sems):
    return [pltpu.make_async_copy(a, b, sems.at[i]) for i, (a, b) in enumerate(pairs)]


def begin(pairs, sems):
    for c in copies(pairs, sems):
        c.start()


def finish(pairs, sems):
    for c in copies(pairs, sems):
        c.wait()


def begin_tiles(pairs_of, count, sems):
    @pl.loop(0, count)
    def _(i):
        begin(pairs_of(i), sems.at[i])


def finish_tiles(pairs_of, count, sems):
    @pl.loop(0, count)
    def _(i):
        finish(pairs_of(i), sems.at[i])


def row_pairs(chunks, held, cols):
    pairs, at = [], 0
    for c in chunks:
        n = c.shape[0]
        pairs.append((c.at[:, cols], held.at[pl.ds(at, n), cols]))
        at += n
    return pairs


def ranks(row):
    n = row.shape[1]
    sub, lane = iota((n, n), 0), iota((n, n), 1)
    col = jnp.sum(jnp.where(sub == lane, row, 0.0), axis=1, keepdims=True)
    same = jnp.where((col == row) & (sub < lane), 1.0, 0.0)
    return jnp.sum(same, axis=0, keepdims=True).astype(I32)


HEAD = 16
BOTH = 2 * CAP


def pack_kernel(where, meta, x, g, out, xv, gv, sems):
    width = xv.shape[1]
    part = width // 4
    tiles = width // TILE
    total, rows = out.shape[0], xv.shape[0]

    def loads(i):
        return [(x.at[:, tile(i)], xv.at[:, tile(i)]), (g.at[:, tile(i)], gv.at[:, tile(i)])]

    begin_tiles(loads, tiles, sems)
    row = meta[0:1, :]
    gate = meta[1:2, :]
    ids = row.astype(I32)
    j = ranks(row) + jnp.where((ids & 1) == where[0] // 2, 0, CAP)
    base = (ids >> 1) * HEAD
    q = iota((total, rows), 0)
    put_x = hot(q == base + j)
    at = jnp.where(j < HEAD - BOTH, base + BOTH + j, -1)
    put_g = jnp.where(q == at, gate, 0.0).astype(BF16)

    @pl.loop(0, tiles)
    def _(i):
        finish(loads(i), sems.at[i])
        cols = tile(i)
        out[:, cols] = (dot(put_x, xv[:, cols]) + dot(put_g, gv[:, cols])).astype(BF16)

    last = None
    for kp in range(4):
        at = jnp.where(j < HEAD - BOTH, -1, base + (j - HEAD + BOTH) * 4 + kp)
        put_t = jnp.where(q == at, gate, 0.0).astype(BF16)
        term = dot(put_t, gv[:, kp * part : (kp + 1) * part])
        last = term if last is None else last + term
    out[:, width:] = last.astype(BF16)


def pack(where, meta, x, g, nodes):
    rows, width = x.shape
    total = nodes * HEAD
    return call(
        "pack",
        pack_kernel,
        [((total, width + width // 4), BF16)],
        [where, meta, x, g],
        [SMEM, VMEM, ANY, ANY],
        [
            pltpu.VMEM((rows, width), BF16),
            pltpu.VMEM((rows, width), BF16),
            pltpu.SemaphoreType.DMA((width // TILE, 2)),
        ],
        2 * total * 3 * rows * width,
    )[0]


def regroup_kernel(msg, near, far):
    total = msg.shape[0]
    width = near.shape[1] // 2
    part = width // 4
    rows = near.shape[0]
    d, q = iota((rows, total), 0), iota((rows, total), 1)
    n = (d * 205) >> 10
    for r, out in enumerate((near, far)):
        j = d - n * CAP + r * CAP
        base = n * HEAD
        get_x = hot(q == base + j)
        get_g = hot((j < HEAD - BOTH) & (q == base + BOTH + j))
        for kp in range(4):
            cols = slice(kp * part, (kp + 1) * part)
            gcols = slice(width + kp * part, width + (kp + 1) * part)
            block = msg[:, cols]
            out[:, cols] = dot(get_x, block).astype(BF16)
            total_g = dot(get_g, block)
            if r == 1:
                get_t = hot((j >= HEAD - BOTH) & (q == base + (j - HEAD + BOTH) * 4 + kp))
                total_g = total_g + dot(get_t, msg[:, width:])
            out[:, gcols] = total_g.astype(BF16)


def regroup(msg, nodes, width):
    return call(
        "regroup",
        regroup_kernel,
        [((nodes * CAP, 2 * width), BF16)] * 2,
        [msg],
        [VMEM],
        [],
        2 * 5 * nodes * CAP * msg.shape[0] * width,
    )


def activations(pre_gate, pre_up, dhidden):
    sig = jax.nn.sigmoid(pre_gate)
    active = pre_gate * sig
    hidden = (active * pre_up).astype(BF16)
    up_in = (dhidden * active).astype(BF16)
    gate_in = (dhidden * pre_up * sig * (1.0 + pre_gate * (1.0 - sig))).astype(BF16)
    return hidden, up_in, gate_in


def weight_pairs(refs, wg, wu, wd, cols):
    go, gs, uo, us, do, ds = refs
    h = do.shape[0]
    own, other = pl.ds(0, h), pl.ds(h, h)
    return [
        (go.at[cols, :], wg.at[cols, own]),
        (gs.at[cols, :], wg.at[cols, other]),
        (uo.at[cols, :], wu.at[cols, own]),
        (us.at[cols, :], wu.at[cols, other]),
        (do.at[:, cols], wd.at[own, cols]),
        (ds.at[:, cols], wd.at[other, cols]),
    ]


def stacked_pairs(refs, wg, wu, wd, cols, i):
    g, u, d, came = refs
    h = d.shape[0]
    own, other = pl.ds(0, h), pl.ds(h, h)
    pairs = [
        (g.at[cols, :], wg.at[cols, own]),
        (came.at[cols, pl.ds(0, h)], wg.at[cols, other]),
        (u.at[cols, :], wu.at[cols, own]),
        (came.at[cols, pl.ds(h, h)], wu.at[cols, other]),
        (d.at[:, cols], wd.at[own, cols]),
    ]
    for c in range(TILE // h):
        at = pl.ds(pl.multiple_of(i * TILE + c * h, h), h)
        pairs.append((came.at[at, pl.ds(2 * h, h)], wd.at[other, at]))
    return pairs


def stack_kernel(g, u, d, out):
    h = g.shape[1]
    out[:, 0:h] = g[...]
    out[:, h : 2 * h] = u[...]
    for c in range(d.shape[1] // h):
        out[c * h : (c + 1) * h, 2 * h :] = d[:, c * h : (c + 1) * h]


def stack(g, u, d):
    width, h = g.shape
    return call("stack", stack_kernel, [((width, 3 * h), BF16)], [g, u, d], [VMEM] * 3, [], 0)[0]


def forward(xv, gv, wg, wu, wd, pg, pu, dh, arrive):
    pg[...] = jnp.zeros_like(pg)
    pu[...] = jnp.zeros_like(pu)
    dh[...] = jnp.zeros_like(dh)

    @pl.loop(0, xv.shape[1] // TILE)
    def _(i):
        arrive(i)
        cols = tile(i)
        x = xv[:, cols]
        pg[...] += dot(x, wg[cols, :])
        pu[...] += dot(x, wu[cols, :])
        dh[...] += dot(gv[:, cols], wd[:, cols], 1, 1)

    return activations(pg[...], pu[...], dh[...])


def shared_rows_kernel(go, uo, came, up_in, gate_in, *refs):
    outs, (wg, wu, held, sems, out_sems) = refs[:4], refs[4:]
    h = go.shape[1]
    own, other = pl.ds(0, h), pl.ds(h, h)

    def loads(i):
        cols = tile(i)
        return [
            (go.at[cols, :], wg.at[cols, own]),
            (came.at[cols, own], wg.at[cols, other]),
            (uo.at[cols, :], wu.at[cols, own]),
            (came.at[cols, other], wu.at[cols, other]),
        ]

    begin_tiles(loads, go.shape[0] // TILE, sems)
    rows_back(gate_in, up_in, wg, wu, outs, held, out_sems, lambda i: finish(loads(i), sems.at[i]))


def rows_back(gate_in, up_in, wg, wu, outs, held, sems, arrive=None):
    rows = outs[0].shape[0]
    tiles = wg.shape[0] // TILE

    def stores(i):
        cols = tile(i)
        return [(held.at[pl.ds(k * rows, rows), cols], o.at[:, cols]) for k, o in enumerate(outs)]

    @pl.loop(0, tiles)
    def _(i):
        if arrive is not None:
            arrive(i)
        cols = tile(i)
        total = dot(gate_in[...], wg[cols, :], 1, 1) + dot(up_in[...], wu[cols, :], 1, 1)
        held[:, cols] = total.astype(BF16)
        begin(stores(i), sems.at[i])

    finish_tiles(stores, tiles, sems)


def shared_rows(weights, up_in, gate_in):
    span, h = up_in.shape
    width = weights[0].shape[0]
    return call(
        "shared_rows",
        shared_rows_kernel,
        [((span // 4, width), BF16)] * 4,
        [weights[0], weights[1], weights[3], up_in, gate_in],
        [ANY] * 3 + [VMEM] * 2,
        [
            pltpu.VMEM((width, h), BF16),
            pltpu.VMEM((width, h), BF16),
            pltpu.VMEM((span, width), BF16),
            pltpu.SemaphoreType.DMA((width // TILE, 4)),
            pltpu.SemaphoreType.DMA((width // TILE, 4)),
        ],
        2 * 2 * span * width * h,
        [ANY] * 4,
    )


def weight_grads(xv, gv, hidden, up_in, gate_in, outs, held, sems, arrive=None):
    tiles = xv.shape[1] // TILE
    h = outs[2].shape[0]
    hg, hu, hd = held

    def stores(i):
        cols = tile(i)
        pairs = []
        for k in range(len(outs) // 3):
            part = pl.ds(k * h, h)
            pairs += [
                (hg.at[cols, part], outs[3 * k].at[cols, :]),
                (hu.at[cols, part], outs[3 * k + 1].at[cols, :]),
                (hd.at[part, cols], outs[3 * k + 2].at[:, cols]),
            ]
        return pairs

    @pl.loop(0, tiles)
    def _(i):
        if arrive is not None:
            arrive(i)
        cols = tile(i)
        x = xv[:, cols]
        hg[cols, :] = dot(x, gate_in[...], 0, 0).astype(BF16)
        hu[cols, :] = dot(x, up_in[...], 0, 0).astype(BF16)
        hd[:, cols] = dot(hidden[...], gv[:, cols], 0, 0).astype(BF16)
        begin(stores(i), sems.at[i])

    finish_tiles(stores, tiles, sems)


def weight_grad_shapes(width, h):
    return [((width, h), BF16), ((width, h), BF16), ((h, width), BF16)] * 2


def shared_weights_kernel(*refs):
    chunks_x, chunks_g, weights = refs[0:7], refs[7:14], refs[14:18]
    outs, up_in, gate_in = refs[18:24], refs[24], refs[25]
    xv, gv, wg, wu, wd, pg, pu, dh, hidden, hg, hu, hd, sems, out_sems = refs[26:]

    def loads(i):
        cols = tile(i)
        return (
            row_pairs(chunks_x, xv, cols)
            + stacked_pairs(weights, wg, wu, wd, cols, i)
            + row_pairs(chunks_g, gv, cols)
        )

    begin_tiles(loads, xv.shape[1] // TILE, sems)
    a, b, c = forward(xv, gv, wg, wu, wd, pg, pu, dh, lambda i: finish(loads(i), sems.at[i]))
    hidden[...] = a
    up_in[...] = b
    gate_in[...] = c
    weight_grads(xv, gv, hidden, up_in, gate_in, outs, (hg, hu, hd), out_sems)


def shared_weights(chunks_x, chunks_g, weights):
    rows, width = chunks_x[0].shape
    span, h = 4 * rows, 2 * weights[0].shape[1]
    outs = call(
        "shared_weights",
        shared_weights_kernel,
        weight_grad_shapes(width, h // 2) + [((span, h), BF16)] * 2,
        [*chunks_x, *chunks_g, *weights],
        [ANY] * 18,
        [
            pltpu.VMEM((span, width), BF16),
            pltpu.VMEM((span, width), BF16),
            pltpu.VMEM((width, h), BF16),
            pltpu.VMEM((width, h), BF16),
            pltpu.VMEM((h, width), BF16),
            pltpu.VMEM((span, h), F32),
            pltpu.VMEM((span, h), F32),
            pltpu.VMEM((span, h), F32),
            pltpu.VMEM((span, h), BF16),
            pltpu.VMEM((width, h), BF16),
            pltpu.VMEM((width, h), BF16),
            pltpu.VMEM((h, width), BF16),
            pltpu.SemaphoreType.DMA((width // TILE, 19 + 2 * TILE // h)),
            pltpu.SemaphoreType.DMA((width // TILE, 6)),
        ],
        2 * 6 * span * width * h,
        [ANY] * 6 + [VMEM] * 2,
    )
    return outs[:6], outs[6], outs[7]


def routed_rows_kernel(n, *refs):
    inputs, weights, refs = refs[:n], refs[n : n + 6], refs[n + 6 :]
    outs, kept, bundle, refs = refs[:n], refs[n : n + 3], refs[n + 3], refs[n + 4 :]
    xv, gv, wg, wu, wd, pg, pu, dh, hidden, up_in, gate_in, rows, sems, o_sems, k_sems = refs
    width = xv.shape[1]
    tiles = width // TILE
    h = kept[0].shape[1]

    def loads(i):
        pairs = weight_pairs(weights, wg, wu, wd, tile(i))
        gcols = pl.ds(pl.multiple_of(width + i * TILE, TILE), TILE)
        for k, b in enumerate(inputs):
            at = pl.ds(k * b.shape[0], b.shape[0])
            pairs.append((b.at[:, tile(i)], xv.at[at, tile(i)]))
            pairs.append((b.at[:, gcols], gv.at[at, tile(i)]))
        return pairs

    begin_tiles(loads, tiles, sems)
    a, b, c = forward(xv, gv, wg, wu, wd, pg, pu, dh, lambda i: finish(loads(i), sems.at[i]))
    hidden[...] = a
    up_in[...] = b
    gate_in[...] = c
    stores = [(xv, bundle.at[:, pl.ds(0, width)]), (gv, bundle.at[:, pl.ds(width, width)])]
    for k, v in enumerate((hidden, up_in, gate_in)):
        stores.append((v.at[:, pl.ds(0, h)], kept[k]))
        stores.append((v.at[:, pl.ds(h, h)], bundle.at[:, pl.ds(2 * width + k * h, h)]))
    begin(stores, k_sems)
    rows_back(gate_in, up_in, wg, wu, outs, rows, o_sems)
    finish(stores, k_sems)


def routed_rows(tag, inputs, weights):
    width, quarter = weights[0].shape
    h = 2 * quarter
    block = inputs[0].shape[0]
    count = len(inputs)
    span = count * block
    tiles = width // TILE
    outs = [((block, width), BF16)] * count + [((span, quarter), BF16)] * 3
    outs += [((span, 2 * width + 3 * quarter), BF16)]
    outs = call(
        "routed_rows" + tag,
        functools.partial(routed_rows_kernel, count),
        outs,
        [*inputs, *weights],
        [ANY] * (count + 6),
        [
            pltpu.VMEM((span, width), BF16),
            pltpu.VMEM((span, width), BF16),
            pltpu.VMEM((width, h), BF16),
            pltpu.VMEM((width, h), BF16),
            pltpu.VMEM((h, width), BF16),
            pltpu.VMEM((span, h), F32),
            pltpu.VMEM((span, h), F32),
            pltpu.VMEM((span, h), F32),
            pltpu.VMEM((span, h), BF16),
            pltpu.VMEM((span, h), BF16),
            pltpu.VMEM((span, h), BF16),
            pltpu.VMEM((span, width), BF16),
            pltpu.SemaphoreType.DMA((tiles, 6 + 2 * count)),
            pltpu.SemaphoreType.DMA((tiles, count)),
            pltpu.SemaphoreType.DMA((8,)),
        ],
        2 * 5 * span * width * h,
        [ANY] * len(outs),
    )
    return outs[:count], outs[count : count + 3], outs[count + 3]


def routed_weights_kernel(*refs):
    bundles, kept, outs = refs[0:4], (refs[4:7], refs[7:10]), refs[10:13]
    xv, gv, hidden, up_in, gate_in, hg, hu, hd, sems, w_sems, o_sems = refs[13:]
    width = xv.shape[1]
    h = kept[0][0].shape[1]
    inner, at = [], 0
    for i in range(4):
        n = bundles[i].shape[0]
        for k, v in enumerate((hidden, up_in, gate_in)):
            if i < 2:
                source = kept[i][k]
            else:
                source = bundles[i].at[:, pl.ds(2 * width + k * h, h)]
            inner.append((source, v.at[pl.ds(at, n)]))
        at += n

    def loads(i):
        pairs, at = [], 0
        for b in bundles:
            n = b.shape[0]
            gcols = pl.ds(pl.multiple_of(width + i * TILE, TILE), TILE)
            pairs.append((b.at[:, tile(i)], xv.at[pl.ds(at, n), tile(i)]))
            pairs.append((b.at[:, gcols], gv.at[pl.ds(at, n), tile(i)]))
            at += n
        return pairs

    begin(inner, sems)
    begin_tiles(loads, width // TILE, w_sems)
    finish(inner, sems)
    arrive = lambda i: finish(loads(i), w_sems.at[i])
    weight_grads(xv, gv, hidden, up_in, gate_in, outs, (hg, hu, hd), o_sems, arrive)


def routed_weights(own, other, kept, width):
    h = kept[0][0].shape[1]
    span = sum(b.shape[0] for b in (*own, *other))
    tiles = width // TILE
    return call(
        "routed_weights",
        routed_weights_kernel,
        weight_grad_shapes(width, h)[:3],
        [*own, *other, *kept[0], *kept[1]],
        [ANY] * 10,
        [
            pltpu.VMEM((span, width), BF16),
            pltpu.VMEM((span, width), BF16),
            pltpu.VMEM((span, h), BF16),
            pltpu.VMEM((span, h), BF16),
            pltpu.VMEM((span, h), BF16),
            pltpu.VMEM((width, h), BF16),
            pltpu.VMEM((width, h), BF16),
            pltpu.VMEM((h, width), BF16),
            pltpu.SemaphoreType.DMA((12,)),
            pltpu.SemaphoreType.DMA((tiles, 8)),
            pltpu.SemaphoreType.DMA((tiles, 3)),
        ],
        2 * 3 * span * width * h,
        [ANY] * 3,
    )


def grad_pack_kernel(g0, u0, d0, g1, u1, d1, out):
    h = g0.shape[1]
    out[:, 0:h] = (g0[...].astype(F32) + g1[...].astype(F32)).astype(BF16)
    out[:, h : 2 * h] = (u0[...].astype(F32) + u1[...].astype(F32)).astype(BF16)
    for c in range(d0.shape[1] // h):
        cols = slice(c * h, (c + 1) * h)
        block = d0[:, cols].astype(F32) + d1[:, cols].astype(F32)
        out[cols, 2 * h :] = block.astype(BF16)


def grad_pack(own, other):
    width, h = own[0].shape
    return call("grad_pack", grad_pack_kernel, [((width, 3 * h), BF16)], [*own, *other], [VMEM] * 6, [], 3 * width * h)[0]


def grad_sum_kernel(came, out):
    total = came[0].astype(F32)
    for n in range(1, came.shape[0]):
        total = total + came[n].astype(F32)
    total = total.astype(BF16)
    for n in range(came.shape[0]):
        out[n] = total


def grad_sum(came, nodes):
    shape = (nodes, came.shape[0] // nodes, came.shape[1])
    out = call("grad_sum", grad_sum_kernel, [(shape, BF16)], [came.reshape(shape)], [VMEM], [], came.size)[0]
    return out


def grad_unpack_kernel(came, g, u, d):
    h = g.shape[1]
    g[...] = came[:, 0:h]
    u[...] = came[:, h : 2 * h]
    for c in range(d.shape[1] // h):
        d[:, c * h : (c + 1) * h] = came[c * h : (c + 1) * h, 2 * h :]


def grad_unpack(came, width, h):
    outs = [((width, h), BF16), ((width, h), BF16), ((h, width), BF16)]
    return call("grad_unpack", grad_unpack_kernel, outs, [came], [VMEM], [], 3 * width * h)


def add_kernel(a, b, out):
    out[...] = (a[...].astype(F32) + b[...].astype(F32)).astype(BF16)


def add(a, b):
    return call("add", add_kernel, [(a.shape, BF16)], [a, b], [VMEM] * 2, [], a.size)[0]


def return_kernel(b0, b1, b2, b3, out):
    block, width = b0.shape
    part = width // 4
    nodes = block // CAP
    shape = (nodes * RET, block)
    q, i = iota(shape, 0), iota(shape, 1)
    n, j = q >> 3, q & 7
    own = hot((j < CAP) & (i == n * CAP + j))
    other = hot((j >= CAP) & (i == n * CAP + j - CAP))
    for kp in range(4):
        cols = slice(kp * part, (kp + 1) * part)
        out[:, cols] = (
            dot(own, b0[:, cols]) + dot(own, b1[:, cols]) + dot(other, b2[:, cols]) + dot(other, b3[:, cols])
        ).astype(BF16)
    last = None
    for kp in range(4):
        cols = slice(kp * part, (kp + 1) * part)
        get = hot(((j & 3) == kp) & (i == n * CAP + 3 + (j >> 2)))
        term = dot(get, b2[:, cols]) + dot(get, b3[:, cols])
        last = term if last is None else last + term
    out[:, width:] = last.astype(BF16)


def return_pack(blocks):
    block, width = blocks[0].shape
    nodes = block // CAP
    return call(
        "return_pack",
        return_kernel,
        [((nodes * RET, width + width // 4), BF16)],
        blocks,
        [VMEM] * 4,
        [],
        2 * nodes * RET * 4 * block * width,
    )[0]


def combine_kernel(where, meta, back, p0, p1, p2, p3, out):
    rows, width = out.shape
    part = width // 4
    n = back.shape[0]
    row = meta[0:1, :]
    ids = row.astype(I32)
    j = ranks(row) + jnp.where((ids & 1) == where[0] // 2, 0, CAP)
    node = ids >> 1
    c = iota((n, rows), 0)
    head = hot((j < RET) & (c == node * RET + j))
    for kp in range(4):
        cols = slice(kp * part, (kp + 1) * part)
        last = hot((j >= RET) & (c == node * RET + (j - RET) * 4 + kp))
        total = dot(head, back[:, cols], 0, 0) + dot(last, back[:, width:], 0, 0)
        for p in (p0, p1, p2, p3):
            total = total + p[:, cols].astype(F32)
        out[:, cols] = total.astype(BF16)


def combine(where, meta, back, parts):
    rows, width = parts[0].shape
    return call(
        "combine",
        combine_kernel,
        [((rows, width), BF16)],
        [where, meta, back, *parts],
        [SMEM] + [VMEM] * 6,
        [],
        2 * rows * back.shape[0] * width * 2,
    )[0]


def gather_y(v):
    half = v.shape[0] // 2
    v1 = from_y(v, 1)
    v3 = from_y(v, 3)
    top = from_y(v1[:half], 1)
    bottom = from_y(v3[half:], 3)
    return [v, v1, top, bottom, v3]


def on_device(x, g, ids, gate, eg, eu, ed, sg, su, sd):
    rows, width = x.shape
    nodes = lax.axis_size("z") * lax.axis_size("x")
    ny = lax.axis_size("y")
    y = lax.axis_index("y")
    where = y.astype(I32).reshape(1)

    axes = ("z", "x")

    def exchange(v):
        return lax.all_to_all(v, axes, split_axis=0, concat_axis=0, tiled=True)

    half = rows // 2
    def named(name, f, *args):
        with jax.named_scope(name):
            return f(*args)

    def pairs_y(name, v, order):
        return named(name, lambda v: lax.ppermute(v, "y", list(enumerate(order))), v)

    def partner(name, v):
        return pairs_y(name, v, (1, 0, 3, 2))

    def beside(name, v):
        return pairs_y(name, v, (3, 2, 1, 0))

    def across(name, v):
        return pairs_y(name, v, (2, 3, 0, 1))

    top, bottom = slice(0, rows // 2), slice(rows // 2, rows)
    x1t, x3b = named("x1t", from_y, x[top], 1), named("x3b", from_y, x[bottom], 3)
    g1t, g3b = named("g1t", from_y, g[top], 1), named("g3b", from_y, g[bottom], 3)
    x1b, x3t = named("x1b", from_y, x[bottom], 1), named("x3t", from_y, x[top], 3)
    g1b, g3t = named("g1b", from_y, g[bottom], 1), named("g3t", from_y, g[top], 3)
    meta = jnp.concatenate([ids.reshape(1, rows).astype(F32), gate.reshape(1, rows).astype(F32)], 0)
    send = pack(where, meta, after(x, x1t, x3b, g1t, g3b), g, nodes)
    x2 = [named("xt", from_y, after(x1t, send), 1), named("xb", from_y, after(x3b, send), 3)]
    g2 = [named("gt", from_y, after(g1t, send), 1), named("gb", from_y, after(g3b, send), 3)]
    xs, gs = [x, x1t, x1b, *x2, x3t, x3b], [g, g1t, g1b, *g2, g3t, g3b]
    msg = named("msg", exchange, send)
    stacked = stack(sg, su, sd)
    shared_w = [sg, su, sd, named("swap_shared", swap_core, stacked)]
    expert_w = []

    grads, up_in, gate_in = shared_weights(xs, gs, shared_w)
    swapped = [named("swap_grads", swap_core, v) for v in grads[3:]]
    for w in (eg[0], eu[0], ed[0]):
        expert_w += [w, named("swap_expert", swap_core, after(w, xs[3]))]
    parts = shared_rows(shared_w, after(up_in, *expert_w[1::2]), gate_in)
    p1, p3 = (named("part", to_y, parts[k], k) for k in (1, 3))
    send = grad_pack([after(grads[0], parts[0]), *grads[1:3]], swapped)
    scattered = named("scatter", exchange, after(send, msg))

    near, far = regroup(after(msg, send), nodes, width)
    r1, r2 = partner("r1", after(near, p1, p3)), beside("r2", after(far, p1, p3))
    r3 = across("r3", after(far, r1, r2))
    (e0, e1, e2), kept0, bundle0 = routed_rows("0", [near, r1, r2], expert_w)
    b1, b2 = partner("b1", e1), beside("b2", e2)
    summed = grad_sum(after(scattered, e0), nodes)
    came = named("gather", exchange, summed.reshape(scattered.shape))
    (e3,), kept1, bundle1 = routed_rows("1", [after(r3, summed)], expert_w)
    b3 = across("b3", e3)
    p2 = named("part", to_y, after(parts[2], e3), 2)
    send = return_pack([after(e0, came), b1, b2, b3])
    returned = named("returned", exchange, after(send, came))
    own = [bundle0, bundle1]
    other = [named("swap_bundle", swap_core, after(b, send)) for b in own]
    e_gate, e_up, e_down = routed_weights(own, other, [kept0, kept1], width)
    g_gate, g_up, g_down = grad_unpack(came, width, sg.shape[1])
    out = combine(where, meta, after(returned, g_gate, e_gate), [parts[0], p1, p2, p3])
    return (out, e_gate[None], e_up[None], e_down[None], g_gate, g_up, g_down)


def solution(mesh):
    whole = Mesh(mesh.devices.reshape(4, 4, 4, 2), ("z", "x", "y", "c"))
    every, local = ("z", "x", "y", "c"), ("y", "c")
    specs = dict(
        rows=P(every, None), expert=P(every, None, None), columns=P(None, local), down=P(local, None)
    )
    return jax.shard_map(
        on_device,
        mesh=whole,
        in_specs=(
            specs["rows"],
            specs["rows"],
            specs["rows"],
            specs["rows"],
            specs["expert"],
            specs["expert"],
            specs["expert"],
            specs["columns"],
            specs["columns"],
            specs["down"],
        ),
        out_specs=(
            specs["rows"],
            specs["expert"],
            specs["expert"],
            specs["expert"],
            specs["columns"],
            specs["columns"],
            specs["down"],
        ),
        check_vma=False,
    )
```
